32 devices in a mesh: groups: 2 (over x), row: 8 (over z, y), col: 2 (over core).
Axes of the slice: x: 2, y: 2, z: 4, core: 2. Of those that a mesh axis runs over, the one named last changes fastest.
Arguments:
- node_features: bfloat16 [32768, 256], P(('groups', 'row', 'col')), parts along dimension 0, may hold values from -6 to 6
- tile_rows: int32 [16, 2, 384], P(('groups', 'row'), 'col'), parts along dimension 0, may hold values from 0 to 15, as said below
- tile_cols: int32 [16, 2, 384], P(('groups', 'row'), 'col'), parts along dimension 0, may hold values from 0 to 63
- tile_masks: int32 [16, 2, 384, 128, 8], P(('groups', 'row'), 'col'), parts along dimension 0, may hold values from 0 to 65535
- tile_count: int32 [16, 2], P(('groups', 'row'), 'col'), parts along dimension 0, may hold values from 96 to 384, as said below
- weight_self: bfloat16 [256, 256], replicated, may hold values from -0.375 to 0.375
- weight_neigh: bfloat16 [256, 256], replicated, may hold values from -0.375 to 0.375
- bias_term: float32 [256], replicated, may hold values from -3 to 3
- out_grad: bfloat16 [32768, 256], P(('groups', 'row', 'col')), parts along dimension 0, may hold values from -6 to 6
Outputs:
- node_out: bfloat16 [32768, 256], P(('groups', 'row', 'col')), parts along dimension 0
- feature_grad: bfloat16 [32768, 256], P(('groups', 'row', 'col')), parts along dimension 0
- grad_self: float32 [512, 256], P('groups'), parts along dimension 0
- grad_neigh: float32 [512, 256], P('groups'), parts along dimension 0
- grad_bias: float32 [512], P('groups'), parts along dimension 0
The draws below stay inside these ranges and needn't reach their ends.
There are 2 independent parts, one for each index of `groups`. The reference program is written for one: setup_inputs(seed, part) draws one part's arguments, and reference() takes and returns one part's arrays. A program takes and returns all parts, laid end to end along the dimension named above; an argument that names none is the same for every part. Nothing has to cross between parts.
Inputs may be any that keep to these rules, and one draw needn't show every extreme that they name: The slots of one grid position name distinct (tile_rows, tile_cols) pairs. `tile_count`: in every draw some grid position has all 384 slots live.
All inputs are finite; a program needn't handle non-finite values.
Results may differ from the reference program's by a relative error of at most 0.0065.
Values may be sent and summed in bfloat16 or wider, within the bound.
No kernel may reach another device: no remote copies, remote signals or barrier semaphores. Data moves between devices by JAX's collectives and lax.ppermute only.
A program may use at most 128 MiB of HBM per device.

```python
from functools import partial
import jax
import jax.numpy as jnp
from jax import lax

FEAT = 256
NODE_DEV = 1024
TILE_SLOTS = 384
NODES = 16384
BLOCK_ROWS = 16
BLOCK_COLS = 64
N_ROW = 8
N_COL = 2


def tile_layout(key):
    layout_key = jax.random.fold_in(key, 11)
    device_keys = jax.random.split(layout_key, N_ROW * N_COL)
    chosen = jax.vmap(lambda one_key: jax.random.permutation(one_key, BLOCK_ROWS * BLOCK_COLS)[:TILE_SLOTS])(device_keys)
    chosen = chosen.astype(jnp.int32).reshape(N_ROW, N_COL, TILE_SLOTS)
    return (chosen // BLOCK_COLS, chosen % BLOCK_COLS)


def draw_tile_rows(key, part):
    return tile_layout(key)[0]


def draw_tile_cols(key, part):
    return tile_layout(key)[1]


def draw_tile_masks(key, part):
    layout_rows = tile_layout(key)[0]
    key = jax.random.fold_in(key, 7)
    node_alive = (jax.random.randint(jax.random.fold_in(key, 1), (N_ROW, BLOCK_ROWS, 128), 0, 8) != 0).astype(jnp.int32)
    grid_index = jnp.arange(N_ROW, dtype=jnp.int32)[:, None, None]
    alive_rows = node_alive[grid_index, layout_rows]
    word_shape = (N_ROW, N_COL, TILE_SLOTS, 128, 8)
    mask_words = jnp.full(word_shape, 65535, jnp.int32)
    for draw_turn in range(8):
        fresh = jax.random.randint(jax.random.fold_in(key, 20 + draw_turn), word_shape, 0, 65536)
        mask_words = jnp.bitwise_and(mask_words, fresh.astype(jnp.int32))
    mask_words = mask_words * alive_rows[..., None]
    return mask_words.at[0, 0, 0, 0, 0].set(65535).astype(jnp.int32)


def draw_tile_count(key, part):
    key = jax.random.fold_in(key, 5)
    positions = N_ROW * N_COL
    counts = jax.random.randint(jax.random.fold_in(key, 1), (positions,), TILE_SLOTS // 4, TILE_SLOTS + 1)
    fullest = jax.random.randint(jax.random.fold_in(key, 2), (), 0, positions)
    counts = jnp.where(jnp.arange(positions, dtype=jnp.int32) == fullest, TILE_SLOTS, counts)
    return counts.astype(jnp.int32).reshape(N_ROW, N_COL)


def block_scale(stream_key, extent, cuts, low, high):
    factor_of, own = 1.0, jax.random.fold_in(stream_key, 6)
    for dim, shards_of in cuts:
        draws = jnp.exp(jax.random.uniform(jax.random.fold_in(own, dim), (shards_of,), jnp.float32, low / len(cuts), high / len(cuts)))
        factor_of = factor_of * jnp.repeat(draws, extent[dim] // shards_of).reshape([-1 if axis == dim else 1 for axis in range(len(extent))])
    return factor_of


def centred(rng, shape, scale, bound, shards=(), kind=jnp.bfloat16):
    entries = jax.random.normal(rng, shape, jnp.float32) * scale
    if len(shards) > 0:
        entries = block_scale(rng, shape, shards, -0.22, 0.18) * entries
    return jnp.clip(entries, min=-bound, max=bound).astype(kind)


def setup_inputs(seed: int = 0, part: int = 0) -> dict:
    splits = jax.random.split(jax.random.key(seed), 10)
    part_splits = jax.random.split(jax.random.fold_in(splits[9], part), 10)
    node_features = centred(part_splits[0], (NODES, FEAT), 1.0, 6.0, ((0, 16),))
    tile_rows = draw_tile_rows(jax.random.fold_in(jax.random.fold_in(splits[9], part), 71), part)
    tile_cols = draw_tile_cols(jax.random.fold_in(jax.random.fold_in(splits[9], part), 71), part)
    tile_masks = draw_tile_masks(jax.random.fold_in(jax.random.fold_in(splits[9], part), 71), part)
    tile_count = draw_tile_count(jax.random.fold_in(jax.random.fold_in(splits[9], part), 71), part)
    weight_self = centred(splits[5], (FEAT, FEAT), FEAT ** -0.5, 0.375)
    weight_neigh = centred(splits[6], (FEAT, FEAT), FEAT ** -0.5, 0.375)
    bias_term = centred(splits[7], (FEAT,), 0.5, 3.0, (), jnp.float32)
    out_grad = centred(part_splits[8], (NODES, FEAT), 1.0, 6.0, ((0, 16),))
    return {"node_features": node_features, "tile_rows": tile_rows, "tile_cols": tile_cols, "tile_masks": tile_masks, "tile_count": tile_count, "weight_self": weight_self, "weight_neigh": weight_neigh, "bias_term": bias_term, "out_grad": out_grad}


def unpack_tiles(mask_words):
    bit_shifts = jnp.arange(16, dtype=jnp.int32)
    bit_values = jnp.bitwise_and(jnp.right_shift(mask_words[..., None], bit_shifts), 1)
    return bit_values.reshape(mask_words.shape[:-2] + (128, 128))

def live_tiles(mask_words, live_total):
    live_flags = (jnp.arange(mask_words.shape[0], dtype=jnp.int32) < live_total).astype(jnp.float32)
    return unpack_tiles(mask_words).astype(jnp.float32) * live_flags[:, None, None]

def reference(node_features, tile_rows, tile_cols, tile_masks, tile_count, weight_self, weight_neigh, bias_term, out_grad):
    positions = N_ROW * N_COL
    row_flat = tile_rows.reshape(positions, TILE_SLOTS)
    col_flat = tile_cols.reshape(positions, TILE_SLOTS)
    mask_flat = tile_masks.reshape(positions, TILE_SLOTS, 128, 8)
    count_flat = tile_count.reshape(positions)
    column_of = (jnp.arange(positions, dtype=jnp.int32) % N_COL).astype(jnp.int32)
    grid_of = (jnp.arange(positions, dtype=jnp.int32) // N_COL).astype(jnp.int32)
    by_block = node_features.reshape(N_ROW, N_COL, NODE_DEV, FEAT)

    def forward_position(inputs):
        row_index, col_index, mask_words, live_total, column = inputs
        tile_block = live_tiles(mask_words, live_total)
        column_nodes = lax.dynamic_index_in_dim(by_block, column, 1, keepdims=False)
        feature_blocks = column_nodes.reshape(BLOCK_COLS, 128, FEAT)[col_index].astype(jnp.float32)
        products = jnp.einsum('gtu,guf->gtf', tile_block, feature_blocks)
        totals = jnp.zeros((BLOCK_ROWS, 128, FEAT), jnp.float32).at[row_index].add(products)
        degrees = jnp.zeros((BLOCK_ROWS, 128), jnp.float32).at[row_index].add(lax.optimization_barrier(jnp.sum(tile_block, axis=2)))
        return (totals, degrees)
    totals, degrees = lax.map(forward_position, (row_flat, col_flat, mask_flat, count_flat, column_of))
    aggregated = lax.optimization_barrier(jnp.sum(totals.reshape(N_ROW, N_COL, N_COL * NODE_DEV, FEAT), axis=1)).reshape(NODES, FEAT)
    degree = lax.optimization_barrier(jnp.sum(degrees.reshape(N_ROW, N_COL, N_COL * NODE_DEV), axis=1)).reshape(NODES)
    divisor = jnp.maximum(degree, 1.0)[:, None]
    neighbour_mean = (aggregated / divisor).astype(jnp.bfloat16)
    pre = jnp.dot(node_features, weight_self, preferred_element_type=jnp.float32)
    pre = pre + jnp.dot(neighbour_mean, weight_neigh, preferred_element_type=jnp.float32)
    pre = pre + bias_term.astype(jnp.float32)
    activate = partial(jax.nn.gelu, approximate=True)
    activated, pullback = jax.vjp(activate, pre)
    node_out = activated.astype(jnp.bfloat16)
    pre_grad = pullback(out_grad.astype(jnp.float32))[0]
    grad_b = pre_grad.astype(jnp.bfloat16)
    grad_scale = NODES ** (-0.5)
    grad_self = jnp.dot(node_features.T, grad_b, preferred_element_type=jnp.float32) * grad_scale
    grad_neigh = jnp.dot(neighbour_mean.T, grad_b, preferred_element_type=jnp.float32) * grad_scale
    grad_bias = lax.optimization_barrier(jnp.sum(pre_grad, axis=0)) * grad_scale
    mean_grad = (jnp.dot(grad_b, weight_neigh.T, preferred_element_type=jnp.float32) / divisor).astype(jnp.bfloat16)
    rows_by_grid = mean_grad.reshape(N_ROW, BLOCK_ROWS, 128, FEAT)

    def backward_position(carry, inputs):
        row_index, col_index, mask_words, live_total, column, grid = inputs
        tile_block = live_tiles(mask_words, live_total)
        grad_blocks = lax.dynamic_index_in_dim(rows_by_grid, grid, 0, keepdims=False)[row_index].astype(jnp.float32)
        products = jnp.einsum('gtu,gtf->guf', tile_block, grad_blocks)
        term = jnp.zeros((BLOCK_COLS, 128, FEAT), jnp.float32).at[col_index].add(products)
        term = term.reshape(N_ROW, NODE_DEV, FEAT)
        current = lax.dynamic_index_in_dim(carry, column, 1, keepdims=False)
        carry = lax.dynamic_update_index_in_dim(carry, current + term, column, 1)
        return (carry, None)
    start_carry = jnp.zeros((N_ROW, N_COL, NODE_DEV, FEAT), jnp.float32)
    summed, unused = lax.scan(backward_position, start_carry, (row_flat, col_flat, mask_flat, count_flat, column_of, grid_of))
    neighbour_grad = summed.reshape(NODES, FEAT)
    feature_grad = (jnp.dot(grad_b, weight_self.T, preferred_element_type=jnp.float32) + neighbour_grad).astype(jnp.bfloat16)
    return (node_out, feature_grad, grad_self, grad_neigh, grad_bias)
```

```python
from functools import partial
import math

import jax
import jax.numpy as jnp
from jax import lax
from jax.experimental import pallas as pl
from jax.experimental.pallas import tpu as pltpu
from jax.sharding import PartitionSpec as P

VMEM_LIMIT = 48 * 1024 * 1024
GELU_C = math.sqrt(2.0 / math.pi)
F32 = jnp.float32
BF16 = jnp.bfloat16


def ring_order(n):
    return list(range(0, n, 2)) + list(range(n - 1, 0, -2))


def unpack_kernel(block_rows, table_ref, masks_ref, out_ref):
    c = pl.program_id(0)
    bit = lax.broadcasted_iota(jnp.int32, (16, 128), 0)
    for r in range(block_rows):
        slot = table_ref[c * block_rows + r]
        words = masks_ref[jnp.maximum(slot, 0)]
        words = jnp.where(slot >= 0, words, 0)
        for k in range(8):
            row = jnp.broadcast_to(words[k : k + 1, :], (16, 128))
            bits = jnp.bitwise_and(jnp.right_shift(row, bit), 1)
            out_ref[16 * k : 16 * k + 16, 128 * r : 128 * r + 128] = bits.astype(F32).astype(BF16)


def unpack(table, masks, block_rows, block_cols):
    return pl.pallas_call(
        partial(unpack_kernel, block_rows),
        grid_spec=pltpu.PrefetchScalarGridSpec(
            num_scalar_prefetch=1,
            grid=(block_cols,),
            in_specs=[pl.BlockSpec(masks.shape, lambda c, t: (0, 0, 0))],
            out_specs=pl.BlockSpec((128, block_rows * 128), lambda c, t: (c, 0)),
        ),
        out_shape=jax.ShapeDtypeStruct((block_cols * 128, block_rows * 128), BF16),
        compiler_params=pltpu.CompilerParams(vmem_limit_bytes=VMEM_LIMIT),
        cost_estimate=pl.CostEstimate(
            flops=0,
            bytes_accessed=block_cols * block_rows * 128 * 128 * 2 + masks.size * 4,
            transcendentals=0,
        ),
        name="unpack_tiles",
    )(table, masks)


def forward_kernel(pieces, has_acc, ids_ref, *refs):
    xs = refs[:pieces]
    bs = refs[pieces : 2 * pieces]
    acc_ref = refs[2 * pieces] if has_acc else None
    out_ref = refs[2 * pieces + int(has_acc)]
    turned = refs[2 * pieces + int(has_acc) + 1]

    @pl.when(pl.program_id(0) == 0)
    def _():
        for k in range(pieces):
            turned[k] = xs[k][...].T

    total = jnp.dot(turned[0], bs[0][...], preferred_element_type=F32)
    for k in range(1, pieces):
        total = total + jnp.dot(turned[k], bs[k][...], preferred_element_type=F32)
    if has_acc:
        total = total + acc_ref[...]
    out_ref[...] = total.astype(out_ref.dtype)


def forward_mm(pieces, ids, dense, acc, first_block, blocks, out_dtype, name):
    rows, width = pieces[0].shape
    count = len(pieces)
    tblk = 512
    scalars = jnp.stack([jnp.asarray(i, jnp.int32) for i in ids] + [jnp.asarray(first_block, jnp.int32)])

    def piece_spec(k):
        return pl.BlockSpec((rows, tblk), lambda t, s: (s[k], s[count] + t))

    in_specs = [pl.BlockSpec((rows, width), lambda t, s: (0, 0)) for _ in range(count)]
    in_specs += [piece_spec(k) for k in range(count)]
    args = list(pieces) + [dense] * count
    if acc is not None:
        in_specs.append(pl.BlockSpec((width, tblk), lambda t, s: (0, s[count] + t)))
        args.append(acc)
    return pl.pallas_call(
        partial(forward_kernel, count, acc is not None),
        grid_spec=pltpu.PrefetchScalarGridSpec(
            num_scalar_prefetch=1,
            grid=(blocks,),
            in_specs=in_specs,
            out_specs=pl.BlockSpec((width, tblk), lambda t, s: (0, t)),
            scratch_shapes=[pltpu.VMEM((count, width, rows), BF16)],
        ),
        out_shape=jax.ShapeDtypeStruct((width, blocks * tblk), out_dtype),
        compiler_params=pltpu.CompilerParams(vmem_limit_bytes=VMEM_LIMIT),
        cost_estimate=pl.CostEstimate(
            flops=2 * count * rows * width * blocks * tblk,
            bytes_accessed=count * rows * blocks * tblk * 2 + 8 * width * blocks * tblk,
            transcendentals=0,
        ),
        name=name,
    )(scalars, *args)


def middle_kernel(
    agg_ref, other_ref, div_ref, x_ref, og_ref, ws_ref, wn_ref, b_ref,
    mean_ref, out_ref, gb_ref, mg_ref, bias_ref,
):
    div = div_ref[...]
    rows = div.shape[1]
    width = x_ref.shape[1]
    mean = ((agg_ref[...] + other_ref[...].astype(F32)) / div).T.astype(BF16)
    mean_ref[...] = mean
    pre = jnp.dot(x_ref[...], ws_ref[...], preferred_element_type=F32)
    pre = pre + jnp.dot(mean, wn_ref[...], preferred_element_type=F32)
    pre = pre + b_ref[...]
    square = pre * pre
    bent = jnp.tanh(GELU_C * (pre + 0.044715 * (square * pre)))
    half = 0.5 * (1.0 + bent)
    out_ref[...] = (pre * half).astype(BF16)
    slope = half + 0.5 * pre * (1.0 - bent * bent) * (GELU_C * (1.0 + 3.0 * 0.044715 * square))
    pre_grad = og_ref[...].astype(F32) * slope
    grad_b = pre_grad.astype(BF16)
    gb_ref[...] = grad_b
    div_column = jnp.broadcast_to(div, (128, rows)).T
    div_full = jnp.concatenate([div_column] * (width // 128), axis=1)
    mean_grad = lax.dot_general(
        grad_b, wn_ref[...], (((1,), (1,)), ((), ())), preferred_element_type=F32
    )
    mg_ref[...] = (mean_grad / div_full).astype(BF16)
    part = jnp.sum(pre_grad.reshape(rows // 8, 8, width), axis=0)

    @pl.when(pl.program_id(0) == 0)
    def _():
        bias_ref[...] = part

    @pl.when(pl.program_id(0) != 0)
    def _():
        bias_ref[...] += part


def middle(agg, other, divisor, x, og, ws, wn, bias):
    rows, width = x.shape
    blk = 256
    turned = pl.BlockSpec((width, blk), lambda i: (0, i))
    plain = pl.BlockSpec((blk, width), lambda i: (i, 0))
    weight = pl.BlockSpec((width, width), lambda i: (0, 0))
    act = jax.ShapeDtypeStruct((rows, width), BF16)
    return pl.pallas_call(
        middle_kernel,
        grid=(rows // blk,),
        in_specs=[
            turned, turned, pl.BlockSpec((1, blk), lambda i: (0, i)), plain, plain, weight, weight,
            pl.BlockSpec((1, width), lambda i: (0, 0)),
        ],
        out_specs=[plain] * 4 + [pl.BlockSpec((8, width), lambda i: (0, 0))],
        out_shape=[act] * 4 + [jax.ShapeDtypeStruct((8, width), F32)],
        compiler_params=pltpu.CompilerParams(vmem_limit_bytes=VMEM_LIMIT),
        cost_estimate=pl.CostEstimate(
            flops=6 * rows * width * width, bytes_accessed=18 * rows * width, transcendentals=rows * width
        ),
        name="layer",
    )(agg, other, divisor, x, og, ws, wn, bias)


def backward_kernel(ids_ref, mine_ref, other_ref, b_mine, b_other, out_ref):
    total = jnp.dot(b_mine[...], mine_ref[...], preferred_element_type=F32)
    out_ref[...] = total + jnp.dot(b_other[...], other_ref[...], preferred_element_type=F32)


def backward_mm(ids, dense, mine, other, side, piece_rows, name):
    rows, width = mine.shape
    count = len(ids)
    scalars = jnp.stack([jnp.asarray(i, jnp.int32) for i in ids] + [side, 1 - side])
    grads = pl.BlockSpec((rows, width), lambda i, s: (0, 0))
    return pl.pallas_call(
        backward_kernel,
        grid_spec=pltpu.PrefetchScalarGridSpec(
            num_scalar_prefetch=1,
            grid=(count,),
            in_specs=[
                grads,
                grads,
                pl.BlockSpec((piece_rows, rows), lambda i, s: (s[i], s[count])),
                pl.BlockSpec((piece_rows, rows), lambda i, s: (s[i], s[count + 1])),
            ],
            out_specs=pl.BlockSpec((piece_rows, width), lambda i, s: (i, 0)),
        ),
        out_shape=jax.ShapeDtypeStruct((count * piece_rows, width), F32),
        compiler_params=pltpu.CompilerParams(vmem_limit_bytes=VMEM_LIMIT),
        cost_estimate=pl.CostEstimate(
            flops=4 * count * piece_rows * rows * width,
            bytes_accessed=4 * count * piece_rows * (rows + width),
            transcendentals=0,
        ),
        name=name,
    )(scalars, mine, other, dense, dense)


def local(
    node_features, tile_rows, tile_cols, tile_masks, tile_count,
    weight_self, weight_neigh, bias_term, out_grad,
):
    node_rows, width = node_features.shape
    n = lax.axis_size("row")
    grid_cols = lax.axis_size("col")
    slots = tile_masks.shape[2]
    block_rows = grid_cols * node_rows // 128
    block_cols = n * node_rows // 128
    half = node_rows // 2
    far = n // 2

    order = ring_order(n)
    clockwise = [(order[k], order[(k + 1) % n]) for k in range(n)]
    counter = [(b, a) for a, b in clockwise]
    swap = [(0, 1), (1, 0)]
    row_id = lax.axis_index("row")
    side = lax.axis_index("col").astype(jnp.int32)
    place_of = [order.index(r) for r in range(n)]
    place = jnp.array(place_of, jnp.int32)[row_id]
    ring = jnp.array(order * 3, jnp.int32)

    def shard_at(offset):
        return ring[place + n + offset]

    low, high = node_features[:half], node_features[half:]
    fl, fh, bl, bh = low, high, low, high
    arrivals = []
    for s in range(1, far):
        fl = lax.ppermute(fl, "row", clockwise)
        bh = lax.ppermute(bh, "row", counter)
        fh = lax.ppermute(fh, "row", clockwise)
        bl = lax.ppermute(bl, "row", counter)
        left, right = shard_at(-s), shard_at(s)
        arrivals.append(([fl, bh, fh, bl], [2 * left, 2 * right + 1, 2 * left + 1, 2 * right]))
    fl = lax.ppermute(fl, "row", clockwise)
    bh = lax.ppermute(bh, "row", counter)
    opposite = shard_at(far)
    last = ([fl, bh], [2 * opposite, 2 * opposite + 1])

    row_index = tile_rows.reshape(slots)
    col_index = tile_cols.reshape(slots)
    masks = jnp.transpose(tile_masks.reshape(slots, 128, 8), (0, 2, 1))
    slot_ids = jnp.arange(slots, dtype=jnp.int32)
    live = slot_ids < tile_count.reshape(())
    keys = jnp.where(live, col_index * block_rows + row_index, -1)
    spots = jnp.arange(block_rows * block_cols, dtype=jnp.int32)
    table = jnp.max(jnp.where(keys[None, :] == spots[:, None], slot_ids[None, :], -1), axis=1)
    dense = unpack(table, masks, block_rows, block_cols)
    counts = jnp.sum(lax.population_count(masks), axis=1).astype(BF16)
    pick = ((jnp.arange(block_rows, dtype=jnp.int32)[:, None] == row_index[None, :]) & live[None, :])
    degree = jnp.dot(pick.astype(BF16), counts, preferred_element_type=F32).reshape(2, 1, node_rows)
    sent_degree = lax.ppermute(lax.dynamic_index_in_dim(degree, 1 - side, 0, False), "col", swap)
    degree = lax.dynamic_index_in_dim(degree, side, 0, False) + sent_degree
    divisor = jnp.maximum(degree, 1.0)

    total_blocks = block_rows * 128 // 512
    own = shard_at(0)
    acc = forward_mm([low, high], [2 * own, 2 * own + 1], dense, None, 0, total_blocks, F32, "forward_own")
    for s, (pieces, ids) in enumerate(arrivals):
        acc = forward_mm(pieces, ids, dense, acc, 0, total_blocks, F32, "forward_step")
    per_side = total_blocks // 2
    for_other = forward_mm(*last, dense, acc, (1 - side) * per_side, per_side, BF16, "forward_send")
    received = lax.ppermute(for_other, "col", swap)
    mine = forward_mm(*last, dense, acc, side * per_side, per_side, F32, "forward_keep")

    mean, node_out, grad_b, mean_grad, bias_part = middle(
        mine, received, divisor, node_features, out_grad, weight_self, weight_neigh,
        bias_term.reshape(1, width),
    )
    other_grad = lax.ppermute(mean_grad, "col", swap)

    terms = backward_mm([2 * opposite, 2 * opposite + 1], dense, mean_grad, other_grad, side, half, "backward_far")
    fl = lax.ppermute(terms[:half].astype(BF16), "row", clockwise)
    bh = lax.ppermute(terms[half:].astype(BF16), "row", counter)
    fh = bl = None
    for s in range(far - 1, 0, -1):
        ahead, behind = shard_at(s), shard_at(-s)
        terms = backward_mm(
            [2 * ahead, 2 * behind + 1, 2 * ahead + 1, 2 * behind],
            dense, mean_grad, other_grad, side, half, "backward_step",
        )
        sums = []
        for k, got in enumerate((fl, bh, fh, bl)):
            part = terms[k * half : (k + 1) * half]
            sums.append((part if got is None else part + got.astype(F32)).astype(BF16))
        fl = lax.ppermute(sums[0], "row", clockwise)
        bh = lax.ppermute(sums[1], "row", counter)
        fh = lax.ppermute(sums[2], "row", clockwise)
        bl = lax.ppermute(sums[3], "row", counter)
    terms = backward_mm([2 * own, 2 * own + 1], dense, mean_grad, other_grad, side, half, "backward_own")
    self_term = lax.dot_general(
        grad_b, weight_self, (((1,), (1,)), ((), ())), preferred_element_type=F32
    )
    rest = terms + self_term
    feature_grad = jnp.concatenate(
        [
            (rest[:half] + fl.astype(F32) + bl.astype(F32)).astype(BF16),
            (rest[half:] + fh.astype(F32) + bh.astype(F32)).astype(BF16),
        ],
        axis=0,
    )

    grad_scale = (node_rows * n * grid_cols) ** (-0.5)
    contract = (((0,), (0,)), ((), ()))
    both = jnp.stack(
        [
            lax.dot_general(node_features, grad_b, contract, preferred_element_type=F32),
            lax.dot_general(mean, grad_b, contract, preferred_element_type=F32),
        ]
    )
    bias_rows = bias_part

    def exchange(send, bias_now, axis, perm):
        got = lax.ppermute(jnp.concatenate([send, bias_now], axis=0), axis, perm)
        return got[: send.shape[0]], bias_now + got[send.shape[0] :]

    got, bias_rows = exchange(
        lax.dynamic_index_in_dim(both, 1 - side, 0, False), bias_rows, "col", swap
    )
    matrix = lax.dynamic_index_in_dim(both, side, 0, False) + got
    bits = int(math.log2(n))
    for b in range(bits):
        perm = [(r, r ^ (1 << b)) for r in range(n)]
        flag = (row_id >> b) & 1
        parts = matrix.reshape(2, matrix.shape[0] // 2, width)
        got, bias_rows = exchange(
            lax.dynamic_index_in_dim(parts, 1 - flag, 0, False), bias_rows, "row", perm
        )
        matrix = lax.dynamic_index_in_dim(parts, flag, 0, False) + got
    for b in reversed(range(bits)):
        perm = [(r, r ^ (1 << b)) for r in range(n)]
        flag = (row_id >> b) & 1
        got = lax.ppermute(matrix, "row", perm)
        matrix = jnp.concatenate(
            [jnp.where(flag == 0, matrix, got), jnp.where(flag == 0, got, matrix)], axis=0
        )
    matrix = matrix * grad_scale
    got = lax.ppermute(matrix, "col", swap)
    grad_self = jnp.where(side == 0, matrix, got)
    grad_neigh = jnp.where(side == 0, got, matrix)
    grad_bias = jnp.sum(bias_rows, axis=0) * grad_scale
    return node_out, feature_grad, grad_self, grad_neigh, grad_bias


def solution(mesh):
    in_specs = (
        P(("groups", "row", "col"), None),
        P(("groups", "row"), "col", None),
        P(("groups", "row"), "col", None),
        P(("groups", "row"), "col", None, None, None),
        P(("groups", "row"), "col"),
        P(),
        P(),
        P(),
        P(("groups", "row", "col"), None),
    )
    out_specs = (
        P(("groups", "row", "col"), None),
        P(("groups", "row", "col"), None),
        P("groups", None),
        P("groups", None),
        P("groups"),
    )
    return jax.shard_map(local, mesh=mesh, in_specs=in_specs, out_specs=out_specs, check_vma=False)
```

```python
from functools import partial
import math

import jax
import jax.numpy as jnp
from jax import lax
from jax.experimental import pallas as pl
from jax.experimental.pallas import tpu as pltpu
from jax.sharding import PartitionSpec as P

VMEM_LIMIT = 14 * 1024 * 1024
BRIEF = pl.CostEstimate(flops=1024, bytes_accessed=1024, transcendentals=0)
GELU_C = math.sqrt(2.0 / math.pi)
F32 = jnp.float32
BF16 = jnp.bfloat16


def ring_order(n):
    return list(range(0, n, 2)) + list(range(n - 1, 0, -2))


def unpack_tile(masks_ref, slot, test):
    words = masks_ref[jnp.maximum(slot, 0)]
    words = jnp.where(slot >= 0, words, 0)
    one, zero = jnp.ones((), BF16), jnp.zeros((), BF16)
    parts = []
    for k in range(8):
        row = jnp.broadcast_to(words[k : k + 1, :], (16, 128)).astype(jnp.int16)
        parts.append(jnp.where(jnp.bitwise_and(row, test) != 0, one, zero))
    return jnp.concatenate(parts, axis=0)


def bit_tests():
    return jnp.left_shift(jnp.ones((), jnp.int16), lax.broadcasted_iota(jnp.int16, (16, 128), 0))


def fill_tiles(table_ref, masks_ref, block_rows, first_col, cols, row_of, tiles, dst):
    test = bit_tests()

    def one_column(c, carry):
        base = (first_col + c) * block_rows
        start = pl.multiple_of(c * 128, 128)
        for r in range(tiles):
            tile = unpack_tile(masks_ref, table_ref[base + row_of(r)], test)
            dst[pl.ds(start, 128), 128 * r : 128 * r + 128] = tile
        return carry

    lax.fori_loop(0, cols, one_column, 0)


def vmem_spec():
    return pl.BlockSpec(memory_space=pltpu.VMEM)


def smem_spec():
    return pl.BlockSpec(memory_space=pltpu.SMEM)


def forward_kernel(cols, side_at, block_rows, tblk, has_acc, ids_ref, table_ref, masks_ref, *refs):
    count = len(cols)
    xs = refs[:count]
    acc_ref = refs[count] if has_acc else None
    out_ref, turned, tiles = refs[count + int(has_acc) :]
    rows = xs[0].shape[0]
    for k in range(count):
        turned[:, k * rows : (k + 1) * rows] = xs[k][...].T
    first = ids_ref[side_at] * out_ref.shape[1] if side_at is not None else 0

    def block(q, carry):
        start = pl.multiple_of(q * tblk, tblk)
        begin = first + start
        first_row = begin // 128
        for k in range(count):
            at, extra = cols[k]
            fill_tiles(
                table_ref, masks_ref, block_rows, ids_ref[at] + extra, rows // 128,
                lambda r: first_row + r, tblk // 128, tiles.at[pl.ds(k * rows, rows)],
            )
        total = jnp.dot(turned[...], tiles[...], preferred_element_type=F32)
        if has_acc:
            total = total + acc_ref[:, pl.ds(pl.multiple_of(begin, tblk), tblk)]
        out_ref[:, pl.ds(start, tblk)] = total.astype(out_ref.dtype)
        return carry

    lax.fori_loop(0, out_ref.shape[1] // tblk, block, 0)


def forward_mm(pieces, cols, side_at, ids, table, masks, acc, out_rows, tblk, block_rows, out_dtype, name):
    rows, width = pieces[0].shape
    count = len(pieces)
    args = [ids, table, masks] + list(pieces) + ([] if acc is None else [acc])
    return pl.pallas_call(
        partial(forward_kernel, tuple(cols), side_at, block_rows, tblk, acc is not None),
        in_specs=[smem_spec(), smem_spec()] + [vmem_spec()] * (len(args) - 2),
        out_specs=vmem_spec(),
        scratch_shapes=[
            pltpu.VMEM((width, count * rows), BF16),
            pltpu.VMEM((count * rows, tblk), BF16),
        ],
        out_shape=jax.ShapeDtypeStruct((width, out_rows), out_dtype),
        compiler_params=pltpu.CompilerParams(vmem_limit_bytes=VMEM_LIMIT),
        cost_estimate=BRIEF,
        name=name,
    )(*args)


def shard_kernel(at, block_rows, ids_ref, table_ref, masks_ref, out_ref):
    fill_tiles(
        table_ref, masks_ref, block_rows, ids_ref[at], out_ref.shape[0] // 128,
        lambda r: r, block_rows, out_ref,
    )


def shard_tiles(at, node_rows, ids, table, masks, block_rows):
    return pl.pallas_call(
        partial(shard_kernel, at, block_rows),
        in_specs=[smem_spec(), smem_spec(), vmem_spec()],
        out_specs=vmem_spec(),
        out_shape=jax.ShapeDtypeStruct((node_rows, block_rows * 128), BF16),
        compiler_params=pltpu.CompilerParams(vmem_limit_bytes=VMEM_LIMIT),
        cost_estimate=BRIEF,
        name="far_tiles",
    )(ids, table, masks)


def last_kernel(at, ids_ref, tiles_ref, low_ref, high_ref, acc_ref, out_ref, turned):
    half = low_ref.shape[0]
    turned[:, :half] = low_ref[...].T
    turned[:, half:] = high_ref[...].T
    rows = out_ref.shape[1]
    columns = pl.ds(pl.multiple_of(ids_ref[at] * rows, rows), rows)
    total = jnp.dot(turned[...], tiles_ref[:, columns], preferred_element_type=F32)
    out_ref[...] = (total + acc_ref[:, columns]).astype(out_ref.dtype)


def last_forward(pieces, at, ids, tiles, acc, out_dtype, name):
    half, width = pieces[0].shape
    rows = acc.shape[1] // 2
    return pl.pallas_call(
        partial(last_kernel, at),
        in_specs=[smem_spec()] + [vmem_spec()] * 4,
        out_specs=vmem_spec(),
        out_shape=jax.ShapeDtypeStruct((width, rows), out_dtype),
        scratch_shapes=[pltpu.VMEM((width, 2 * half), BF16)],
        compiler_params=pltpu.CompilerParams(vmem_limit_bytes=VMEM_LIMIT),
        cost_estimate=BRIEF,
        name=name,
    )(ids, tiles, *pieces, acc)


def first_kernel(at, has_acc, ids_ref, tiles_ref, grad_ref, *refs):
    out_ref = refs[-1]
    rows = grad_ref.shape[0]
    columns = pl.ds(pl.multiple_of(ids_ref[at] * rows, rows), rows)
    total = jnp.dot(tiles_ref[:, columns], grad_ref[...], preferred_element_type=F32)
    if has_acc:
        total = total + refs[0][...]
    out_ref[...] = total.astype(out_ref.dtype)


def first_backward(grad, at, ids, tiles, acc, out_dtype, name):
    rows, width = grad.shape
    args = [ids, tiles, grad] + ([] if acc is None else [acc])
    return pl.pallas_call(
        partial(first_kernel, at, acc is not None),
        in_specs=[smem_spec()] + [vmem_spec()] * (len(args) - 1),
        out_specs=vmem_spec(),
        out_shape=jax.ShapeDtypeStruct((tiles.shape[0], width), out_dtype),
        compiler_params=pltpu.CompilerParams(vmem_limit_bytes=VMEM_LIMIT),
        cost_estimate=BRIEF,
        name=name,
    )(*args)


def middle_kernel(
    agg_ref, other_ref, div_ref, own_ref, og_ref, wn_ref,
    mean_ref, out_ref, gb_ref, mg_ref, bias_ref,
):
    div = div_ref[...]
    rows = div.shape[1]
    width = own_ref.shape[1]
    mean = ((agg_ref[...] + other_ref[...].astype(F32)) / div).T.astype(BF16)
    mean_ref[...] = mean
    pre = own_ref[...] + jnp.dot(mean, wn_ref[...], preferred_element_type=F32)
    square = pre * pre
    bent = jnp.tanh(GELU_C * (pre + 0.044715 * (square * pre)))
    half = 0.5 * (1.0 + bent)
    out_ref[...] = (pre * half).astype(BF16)
    slope = half + 0.5 * pre * (1.0 - bent * bent) * (GELU_C * (1.0 + 3.0 * 0.044715 * square))
    pre_grad = og_ref[...] * slope
    grad_b = pre_grad.astype(BF16)
    gb_ref[...] = grad_b
    div_column = jnp.broadcast_to(div, (128, rows)).T
    div_full = jnp.concatenate([div_column] * (width // 128), axis=1)
    mean_grad = lax.dot_general(
        grad_b, wn_ref[...], (((1,), (1,)), ((), ())), preferred_element_type=F32
    )
    mg_ref[...] = (mean_grad / div_full).astype(BF16)
    part = jnp.sum(pre_grad.reshape(rows // 32, 32, width), axis=0)

    @pl.when(pl.program_id(0) == 0)
    def _():
        bias_ref[...] = part

    @pl.when(pl.program_id(0) != 0)
    def _():
        bias_ref[...] += part


def middle(agg, other, divisor, own, og, wn):
    rows, width = own.shape
    blk = 256
    turned = pl.BlockSpec((width, blk), lambda i: (0, i))
    plain = pl.BlockSpec((blk, width), lambda i: (i, 0))
    weight = pl.BlockSpec((width, width), lambda i: (0, 0))
    act = jax.ShapeDtypeStruct((rows, width), BF16)
    return pl.pallas_call(
        middle_kernel,
        grid=(rows // blk,),
        in_specs=[
            turned, turned, pl.BlockSpec((1, blk), lambda i: (0, i)), plain, plain, weight,
        ],
        out_specs=[plain] * 4 + [pl.BlockSpec((32, width), lambda i: (0, 0))],
        out_shape=[act] * 4 + [jax.ShapeDtypeStruct((32, width), F32)],
        compiler_params=pltpu.CompilerParams(vmem_limit_bytes=VMEM_LIMIT),
        cost_estimate=BRIEF,
        name="layer",
    )(agg, other, divisor, own, og, wn)


def backward_kernel(cols, sides, block_rows, has_acc, ids_ref, table_ref, masks_ref, after_ref, *refs):
    del after_ref
    grads = refs[: len(sides)]
    acc_ref = refs[len(sides)] if has_acc else None
    out_ref, tiles = refs[len(sides) + int(has_acc) :]
    piece_rows = out_ref.shape[0]
    rows = grads[0].shape[0]
    per_side = rows // 128
    first_col = ids_ref[cols[0]]
    for p in range(1, len(cols)):
        first_col = jnp.where(pl.program_id(0) == p, ids_ref[cols[p]], first_col)
    for k, side_at in enumerate(sides):
        base = ids_ref[side_at] * per_side
        fill_tiles(
            table_ref, masks_ref, block_rows, first_col, piece_rows // 128,
            lambda r: base + r, per_side, tiles.at[:, pl.ds(k * rows, rows)],
        )
    total = None
    for k in range(len(sides)):
        term = jnp.dot(
            tiles[:, k * rows : (k + 1) * rows], grads[k][...], preferred_element_type=F32
        )
        total = term if total is None else total + term
    if has_acc:
        total = total + acc_ref[...].astype(F32)
    out_ref[...] = total.astype(out_ref.dtype)


def backward_mm(cols, grads, sides, after, ids, table, masks, acc, piece_rows, block_rows, out_dtype, name):
    rows, width = grads[0].shape
    args = [ids, table, masks, after] + list(grads) + ([] if acc is None else [acc])
    piece = pl.BlockSpec((piece_rows, width), lambda p: (p, 0))
    return pl.pallas_call(
        partial(backward_kernel, tuple(cols), tuple(sides), block_rows, acc is not None),
        grid=(len(cols),),
        in_specs=[smem_spec(), smem_spec(), vmem_spec(), pl.BlockSpec(memory_space=pl.ANY)]
        + [vmem_spec()] * len(grads)
        + ([] if acc is None else [piece]),
        out_specs=piece,
        scratch_shapes=[pltpu.VMEM((piece_rows, len(grads) * rows), BF16)],
        out_shape=jax.ShapeDtypeStruct((len(cols) * piece_rows, width), out_dtype),
        compiler_params=pltpu.CompilerParams(vmem_limit_bytes=VMEM_LIMIT),
        cost_estimate=BRIEF,
        name=name,
    )(*args)


def small_call(kernel, name, out_shape, args):
    return pl.pallas_call(
        kernel,
        in_specs=[smem_spec()] + [vmem_spec()] * (len(args) - 1),
        out_specs=jax.tree.map(lambda _: vmem_spec(), out_shape),
        out_shape=out_shape,
        compiler_params=pltpu.CompilerParams(vmem_limit_bytes=VMEM_LIMIT),
        cost_estimate=BRIEF,
        name=name,
    )(*args)


def weight_kernel(at, ids_ref, x_ref, mean_ref, gb_ref, bias_ref, keep_ref, send_ref):
    width = gb_ref.shape[1]
    grad = gb_ref[...]
    own = jnp.dot(x_ref[...].T, grad, preferred_element_type=F32)
    neigh = jnp.dot(mean_ref[...].T, grad, preferred_element_type=F32)
    first = ids_ref[at] == 0
    keep_ref[:width] = jnp.where(first, own, neigh)
    send_ref[:width] = jnp.where(first, neigh, own)
    keep_ref[width:] = bias_ref[...]
    send_ref[width:] = bias_ref[...]


def split_kernel(at, ids_ref, keep_ref, got_ref, *outs):
    chunk = outs[0].shape[0]
    for x, out in enumerate(outs):
        rows = pl.ds(pl.multiple_of(ids_ref[at + x], 8), chunk)
        out[...] = keep_ref[rows] + got_ref[rows]


def join_kernel(at, scale, ids_ref, *refs):
    out = refs[-1]
    for x, part in enumerate(refs[:-1]):
        rows = pl.ds(pl.multiple_of(ids_ref[at + x], 8), part.shape[0])
        out[rows] = part[...] * scale


def local(
    node_features, tile_rows, tile_cols, tile_masks, tile_count,
    weight_self, weight_neigh, bias_term, out_grad,
):
    node_rows, width = node_features.shape
    n = lax.axis_size("row")
    grid_cols = lax.axis_size("col")
    slots = tile_masks.shape[2]
    block_rows = grid_cols * node_rows // 128
    block_cols = n * node_rows // 128
    half = node_rows // 2
    far = n // 2

    order = ring_order(n)
    clockwise = [(order[k], order[(k + 1) % n]) for k in range(n)]
    counter = [(b, a) for a, b in clockwise]
    swap = [(0, 1), (1, 0)]
    row_id = lax.axis_index("row")
    side = lax.axis_index("col").astype(jnp.int32)
    shard_cols = node_rows // 128
    at_side, at_other, at_quad = n, n + 1, n + 2
    bias_rows = 32
    chunk = (width + bias_rows) // 4
    known = [
        [order[(order.index(r) + k) % n] * shard_cols for k in range(n)]
        + [c, 1 - c]
        + [((r & 3) ^ x) * chunk for x in range(4)]
        for r in range(n)
        for c in range(grid_cols)
    ]
    ids = lax.dynamic_index_in_dim(
        jnp.array(known, jnp.int32), row_id * grid_cols + side, 0, keepdims=False
    )

    row_index = tile_rows.reshape(slots)
    col_index = tile_cols.reshape(slots)
    masks = jnp.transpose(tile_masks.reshape(slots, 128, 8), (0, 2, 1))
    slot_ids = jnp.arange(slots, dtype=jnp.int32)
    live = slot_ids < tile_count.reshape(())
    keys = jnp.where(live, col_index * block_rows + row_index, -1)
    spots = jnp.arange(block_rows * block_cols, dtype=jnp.int32)
    table = jnp.max(jnp.where(keys[None, :] == spots[:, None], slot_ids[None, :], -1), axis=1)
    counts = jnp.sum(lax.population_count(masks), axis=1).astype(BF16)
    pick = ((jnp.arange(block_rows, dtype=jnp.int32)[:, None] == row_index[None, :]) & live[None, :])
    degree = jnp.dot(pick.astype(BF16), counts, preferred_element_type=F32).reshape(2, 1, node_rows)
    sent_degree = lax.ppermute(lax.dynamic_index_in_dim(degree, 1 - side, 0, False), "col", swap)
    degree = lax.dynamic_index_in_dim(degree, side, 0, False) + sent_degree
    divisor = jnp.maximum(degree, 1.0)

    forward = partial(forward_mm, ids=ids, table=table, masks=masks, block_rows=block_rows, tblk=1024)
    row_total = block_rows * 128
    from_left = from_right = node_features
    pieces, cols, acc = [node_features], [(0, 0)], None
    early = (node_features, weight_self, bias_term, out_grad, ids, divisor)
    for s in range(1, far + 1):
        if s < far:
            next_left = lax.ppermute(from_left, "row", clockwise)
            next_right = lax.ppermute(from_right, "row", counter)
            next_cols = [(n - s, 0), (s, 0)]
        else:
            next_left = lax.ppermute(from_left[:half], "row", clockwise)
            next_right = lax.ppermute(from_right[half:], "row", counter)
        acc = forward(
            pieces, cols, None, acc=acc, out_rows=row_total, out_dtype=F32, name="forward_step"
        )
        if s == 2:
            x_now, ws_now, b_now, og_now, ids_now, div_now = early
            own_part = jnp.dot(x_now, ws_now, preferred_element_type=F32) + b_now
            far_tiles = shard_tiles(far, node_rows, ids_now, table, masks, block_rows)
            early = (own_part, og_now.astype(F32), far_tiles, div_now)
        acc, from_left, from_right, early = lax.optimization_barrier((acc, next_left, next_right, early))
        pieces, cols = [from_left, from_right], next_cols
    own_part, wide_out_grad, far_tiles, divisor = early
    for_other = last_forward(pieces, at_other, ids, far_tiles, acc, BF16, "forward_send")
    received = lax.ppermute(for_other, "col", swap)
    mine = last_forward(pieces, at_side, ids, far_tiles, acc, F32, "forward_keep")
    mine, received = lax.optimization_barrier((mine, received))

    mean, node_out, grad_b, mean_grad, bias_part = middle(
        mine, received, divisor, own_part, wide_out_grad, weight_neigh
    )
    other_grad = lax.ppermute(mean_grad, "col", swap)

    backward = partial(
        backward_mm, ids=ids, table=table, masks=masks, piece_rows=node_rows, block_rows=block_rows
    )
    far_terms = first_backward(mean_grad, at_side, ids, far_tiles, None, F32, "backward_far_own")
    far_terms = first_backward(other_grad, at_other, ids, far_tiles, far_terms, BF16, "backward_far")
    both_grads, both_sides = [mean_grad, other_grad], [at_side, at_other]

    grad_scale = (node_rows * n * grid_cols) ** (-0.5)
    bits = int(math.log2(n))

    matrix_shape = jax.ShapeDtypeStruct((4 * chunk, width), F32)

    def quad_perm(x):
        return [(r, r ^ x) for r in range(n)]

    def to_core(parts):
        keep, send = small_call(
            partial(weight_kernel, at_side), "weight_grads", [matrix_shape] * 2, (ids,) + parts
        )
        return keep, lax.ppermute(send, "col", swap)

    def to_quad(parts):
        quarter = jax.ShapeDtypeStruct((chunk, width), F32)
        parts = small_call(partial(split_kernel, at_quad), "split_grads", [quarter] * 4, (ids,) + parts)
        return [parts[0]] + [lax.ppermute(parts[x], "row", quad_perm(x)) for x in (1, 2, 3)]

    def add_all(b, parts):
        quarter = sum(parts[1:], parts[0])
        return [quarter, lax.ppermute(quarter, "row", [(r, r ^ (1 << b)) for r in range(n)])]

    def from_quad(parts):
        quarter = sum(parts[1:], parts[0])
        return [quarter] + [lax.ppermute(quarter, "row", quad_perm(x)) for x in (1, 2, 3)]

    spread = [[] for _ in range(far)]
    spread[0].append(to_core)
    spread[1].append(to_quad)
    for b in range(2, bits):
        spread[b].append(partial(add_all, b))
    spread[far - 1].append(from_quad)

    weights = (node_features, mean, grad_b, bias_part)
    right, left = far_terms[:half], far_terms[half:]
    for s in range(far - 1, -1, -1):
        right, left, grads = lax.optimization_barrier((right, left, both_grads))
        right = lax.ppermute(right, "row", clockwise)
        left = lax.ppermute(left, "row", counter)
        if s > 0:
            terms = backward(
                [s, n - s], grads, both_sides, grads[0], acc=None, out_dtype=BF16, name="backward_step"
            )
        else:
            terms = backward(
                [0], grads, both_sides, grads[0], acc=None, out_dtype=F32, name="backward_own"
            )
            self_term = lax.dot_general(
                grad_b, weight_self, (((1,), (1,)), ((), ())), preferred_element_type=F32
            )
            terms = terms + self_term
        terms, weights = lax.optimization_barrier((terms, weights))
        for one in spread[far - 1 - s]:
            weights = one(weights)
        terms, right, left, both_grads = lax.optimization_barrier((terms, right, left, grads))
        if s > 0:
            if s == far - 1:
                gap = jnp.zeros((half, width), BF16)
                right = jnp.concatenate([right, gap], axis=0)
                left = jnp.concatenate([gap, left], axis=0)
            right = (terms[:node_rows].astype(F32) + right.astype(F32)).astype(BF16)
            left = (terms[node_rows:].astype(F32) + left.astype(F32)).astype(BF16)
        else:
            feature_grad = (terms + right.astype(F32) + left.astype(F32)).astype(BF16)

    matrix = small_call(
        partial(join_kernel, at_quad, grad_scale), "join_grads", matrix_shape, (ids,) + tuple(weights)
    )
    got = lax.ppermute(matrix[:width], "col", swap)
    grad_self = jnp.where(side == 0, matrix[:width], got)
    grad_neigh = jnp.where(side == 0, got, matrix[:width])
    grad_bias = jnp.sum(matrix[width:], axis=0)
    return node_out, feature_grad, grad_self, grad_neigh, grad_bias


def solution(mesh):
    in_specs = (
        P(("groups", "row", "col"), None),
        P(("groups", "row"), "col", None),
        P(("groups", "row"), "col", None),
        P(("groups", "row"), "col", None, None, None),
        P(("groups", "row"), "col"),
        P(),
        P(),
        P(),
        P(("groups", "row", "col"), None),
    )
    out_specs = (
        P(("groups", "row", "col"), None),
        P(("groups", "row", "col"), None),
        P("groups", None),
        P("groups", None),
        P("groups"),
    )
    return jax.shard_map(local, mesh=mesh, in_specs=in_specs, out_specs=out_specs, check_vma=False)
```

```python
from functools import partial
import math

import jax
import jax.numpy as jnp
from jax import lax
from jax.experimental import pallas as pl
from jax.experimental.pallas import tpu as pltpu
from jax.sharding import PartitionSpec as P

VMEM_LIMIT = 14 * 1024 * 1024
BRIEF = pl.CostEstimate(flops=1024, bytes_accessed=1024, transcendentals=0)
GELU_C = math.sqrt(2.0 / math.pi)
F32 = jnp.float32
BF16 = jnp.bfloat16


def ring_order(n):
    return list(range(0, n, 2)) + list(range(n - 1, 0, -2))


def unpack_tile(masks_ref, slot, test):
    words = masks_ref[jnp.maximum(slot, 0)]
    words = jnp.where(slot >= 0, words, 0)
    one, zero = jnp.ones((), BF16), jnp.zeros((), BF16)
    parts = []
    for k in range(8):
        row = jnp.broadcast_to(words[k : k + 1, :], (16, 128)).astype(jnp.int16)
        parts.append(jnp.where(jnp.bitwise_and(row, test) != 0, one, zero))
    return jnp.concatenate(parts, axis=0)


def bit_tests():
    return jnp.left_shift(jnp.ones((), jnp.int16), lax.broadcasted_iota(jnp.int16, (16, 128), 0))


def fill_tiles(table_ref, masks_ref, block_rows, first_col, cols, row_of, tiles, dst):
    test = bit_tests()

    def one_column(c, carry):
        base = (first_col + c) * block_rows
        start = pl.multiple_of(c * 128, 128)
        for r in range(tiles):
            tile = unpack_tile(masks_ref, table_ref[base + row_of(r)], test)
            dst[pl.ds(start, 128), 128 * r : 128 * r + 128] = tile
        return carry

    lax.fori_loop(0, cols, one_column, 0)


def vmem_spec():
    return pl.BlockSpec(memory_space=pltpu.VMEM)


def smem_spec():
    return pl.BlockSpec(memory_space=pltpu.SMEM)


def forward_kernel(cols, side_at, block_rows, tblk, has_acc, ids_ref, table_ref, masks_ref, *refs):
    count = len(cols)
    xs = refs[:count]
    acc_ref = refs[count] if has_acc else None
    out_ref, turned, tiles = refs[count + int(has_acc) :]
    rows = xs[0].shape[0]
    for k in range(count):
        turned[:, k * rows : (k + 1) * rows] = xs[k][...].T
    first = ids_ref[side_at] * out_ref.shape[1] if side_at is not None else 0

    def block(q, carry):
        start = pl.multiple_of(q * tblk, tblk)
        begin = first + start
        first_row = begin // 128
        for k in range(count):
            at, extra = cols[k]
            fill_tiles(
                table_ref, masks_ref, block_rows, ids_ref[at] + extra, rows // 128,
                lambda r: first_row + r, tblk // 128, tiles.at[pl.ds(k * rows, rows)],
            )
        total = jnp.dot(turned[...], tiles[...], preferred_element_type=F32)
        if has_acc:
            total = total + acc_ref[:, pl.ds(pl.multiple_of(begin, tblk), tblk)]
        out_ref[:, pl.ds(start, tblk)] = total.astype(out_ref.dtype)
        return carry

    lax.fori_loop(0, out_ref.shape[1] // tblk, block, 0)


def forward_mm(pieces, cols, side_at, ids, table, masks, acc, out_rows, tblk, block_rows, out_dtype, name):
    rows, width = pieces[0].shape
    count = len(pieces)
    args = [ids, table, masks] + list(pieces) + ([] if acc is None else [acc])
    return pl.pallas_call(
        partial(forward_kernel, tuple(cols), side_at, block_rows, tblk, acc is not None),
        in_specs=[smem_spec(), smem_spec()] + [vmem_spec()] * (len(args) - 2),
        out_specs=vmem_spec(),
        scratch_shapes=[
            pltpu.VMEM((width, count * rows), BF16),
            pltpu.VMEM((count * rows, tblk), BF16),
        ],
        out_shape=jax.ShapeDtypeStruct((width, out_rows), out_dtype),
        compiler_params=pltpu.CompilerParams(vmem_limit_bytes=VMEM_LIMIT),
        cost_estimate=BRIEF,
        name=name,
    )(*args)


def shard_kernel(at, block_rows, ids_ref, table_ref, masks_ref, out_ref):
    fill_tiles(
        table_ref, masks_ref, block_rows, ids_ref[at], out_ref.shape[0] // 128,
        lambda r: r, block_rows, out_ref,
    )


def shard_tiles(at, node_rows, ids, table, masks, block_rows):
    return pl.pallas_call(
        partial(shard_kernel, at, block_rows),
        in_specs=[smem_spec(), smem_spec(), vmem_spec()],
        out_specs=vmem_spec(),
        out_shape=jax.ShapeDtypeStruct((node_rows, block_rows * 128), BF16),
        compiler_params=pltpu.CompilerParams(vmem_limit_bytes=VMEM_LIMIT),
        cost_estimate=BRIEF,
        name="far_tiles",
    )(ids, table, masks)


def last_kernel(at, ids_ref, tiles_ref, low_ref, high_ref, acc_ref, out_ref, turned):
    half = low_ref.shape[0]
    turned[:, :half] = low_ref[...].T
    turned[:, half:] = high_ref[...].T
    rows = out_ref.shape[1]
    columns = pl.ds(pl.multiple_of(ids_ref[at] * rows, rows), rows)
    total = jnp.dot(turned[...], tiles_ref[:, columns], preferred_element_type=F32)
    out_ref[...] = (total + acc_ref[:, columns]).astype(out_ref.dtype)


def last_forward(pieces, at, ids, tiles, acc, out_dtype, name):
    half, width = pieces[0].shape
    rows = acc.shape[1] // 2
    return pl.pallas_call(
        partial(last_kernel, at),
        in_specs=[smem_spec()] + [vmem_spec()] * 4,
        out_specs=vmem_spec(),
        out_shape=jax.ShapeDtypeStruct((width, rows), out_dtype),
        scratch_shapes=[pltpu.VMEM((width, 2 * half), BF16)],
        compiler_params=pltpu.CompilerParams(vmem_limit_bytes=VMEM_LIMIT),
        cost_estimate=BRIEF,
        name=name,
    )(ids, tiles, *pieces, acc)


def first_kernel(at, has_acc, ids_ref, tiles_ref, grad_ref, *refs):
    out_ref = refs[-1]
    rows = grad_ref.shape[0]
    columns = pl.ds(pl.multiple_of(ids_ref[at] * rows, rows), rows)
    total = jnp.dot(tiles_ref[:, columns], grad_ref[...], preferred_element_type=F32)
    if has_acc:
        total = total + refs[0][...]
    out_ref[...] = total.astype(out_ref.dtype)


def first_backward(grad, at, ids, tiles, acc, out_dtype, name):
    rows, width = grad.shape
    args = [ids, tiles, grad] + ([] if acc is None else [acc])
    return pl.pallas_call(
        partial(first_kernel, at, acc is not None),
        in_specs=[smem_spec()] + [vmem_spec()] * (len(args) - 1),
        out_specs=vmem_spec(),
        out_shape=jax.ShapeDtypeStruct((tiles.shape[0], width), out_dtype),
        compiler_params=pltpu.CompilerParams(vmem_limit_bytes=VMEM_LIMIT),
        cost_estimate=BRIEF,
        name=name,
    )(*args)


def middle_kernel(
    agg_ref, other_ref, div_ref, own_ref, og_ref, wn_ref,
    mean_ref, out_ref, gb_ref, mg_ref, bias_ref,
):
    div = div_ref[...]
    rows = div.shape[1]
    width = own_ref.shape[1]
    mean = ((agg_ref[...] + other_ref[...].astype(F32)) / div).T.astype(BF16)
    mean_ref[...] = mean
    pre = own_ref[...] + jnp.dot(mean, wn_ref[...], preferred_element_type=F32)
    square = pre * pre
    bent = jnp.tanh(GELU_C * (pre + 0.044715 * (square * pre)))
    half = 0.5 * (1.0 + bent)
    out_ref[...] = (pre * half).astype(BF16)
    slope = half + 0.5 * pre * (1.0 - bent * bent) * (GELU_C * (1.0 + 3.0 * 0.044715 * square))
    pre_grad = og_ref[...] * slope
    grad_b = pre_grad.astype(BF16)
    gb_ref[...] = grad_b
    div_column = jnp.broadcast_to(div, (128, rows)).T
    div_full = jnp.concatenate([div_column] * (width // 128), axis=1)
    mean_grad = lax.dot_general(
        grad_b, wn_ref[...], (((1,), (1,)), ((), ())), preferred_element_type=F32
    )
    mg_ref[...] = (mean_grad / div_full).astype(BF16)
    part = jnp.sum(pre_grad.reshape(rows // 64, 64, width), axis=0)

    @pl.when(pl.program_id(0) == 0)
    def _():
        bias_ref[...] = part

    @pl.when(pl.program_id(0) != 0)
    def _():
        bias_ref[...] += part


def middle(agg, other, divisor, own, og, wn):
    rows, width = own.shape
    blk = 256
    turned = pl.BlockSpec((width, blk), lambda i: (0, i))
    plain = pl.BlockSpec((blk, width), lambda i: (i, 0))
    weight = pl.BlockSpec((width, width), lambda i: (0, 0))
    act = jax.ShapeDtypeStruct((rows, width), BF16)
    return pl.pallas_call(
        middle_kernel,
        grid=(rows // blk,),
        in_specs=[
            turned, turned, pl.BlockSpec((1, blk), lambda i: (0, i)), plain, plain, weight,
        ],
        out_specs=[plain] * 4 + [pl.BlockSpec((64, width), lambda i: (0, 0))],
        out_shape=[act] * 4 + [jax.ShapeDtypeStruct((64, width), F32)],
        compiler_params=pltpu.CompilerParams(vmem_limit_bytes=VMEM_LIMIT),
        cost_estimate=BRIEF,
        name="layer",
    )(agg, other, divisor, own, og, wn)


def backward_kernel(cols, sides, block_rows, has_acc, ids_ref, table_ref, masks_ref, after_ref, *refs):
    del after_ref
    grads = refs[: len(sides)]
    acc_ref = refs[len(sides)] if has_acc else None
    out_ref, tiles = refs[len(sides) + int(has_acc) :]
    piece_rows = out_ref.shape[0]
    rows = grads[0].shape[0]
    per_side = rows // 128
    first_col = ids_ref[cols[0]]
    for p in range(1, len(cols)):
        first_col = jnp.where(pl.program_id(0) == p, ids_ref[cols[p]], first_col)
    for k, side_at in enumerate(sides):
        base = ids_ref[side_at] * per_side
        fill_tiles(
            table_ref, masks_ref, block_rows, first_col, piece_rows // 128,
            lambda r: base + r, per_side, tiles.at[:, pl.ds(k * rows, rows)],
        )
    total = None
    for k in range(len(sides)):
        term = jnp.dot(
            tiles[:, k * rows : (k + 1) * rows], grads[k][...], preferred_element_type=F32
        )
        total = term if total is None else total + term
    if has_acc:
        total = total + acc_ref[...].astype(F32)
    out_ref[...] = total.astype(out_ref.dtype)


def backward_mm(cols, grads, sides, after, ids, table, masks, acc, piece_rows, block_rows, out_dtype, name):
    rows, width = grads[0].shape
    args = [ids, table, masks, after] + list(grads) + ([] if acc is None else [acc])
    piece = pl.BlockSpec((piece_rows, width), lambda p: (p, 0))
    return pl.pallas_call(
        partial(backward_kernel, tuple(cols), tuple(sides), block_rows, acc is not None),
        grid=(len(cols),),
        in_specs=[smem_spec(), smem_spec(), vmem_spec(), pl.BlockSpec(memory_space=pl.ANY)]
        + [vmem_spec()] * len(grads)
        + ([] if acc is None else [piece]),
        out_specs=piece,
        scratch_shapes=[pltpu.VMEM((piece_rows, len(grads) * rows), BF16)],
        out_shape=jax.ShapeDtypeStruct((len(cols) * piece_rows, width), out_dtype),
        compiler_params=pltpu.CompilerParams(vmem_limit_bytes=VMEM_LIMIT),
        cost_estimate=pl.CostEstimate(
            flops=8 * len(cols) * piece_rows * rows * len(grads) * width,
            bytes_accessed=masks.size * 4 + 4 * len(cols) * piece_rows * width,
            transcendentals=0,
        ),
        name=name,
    )(*args)


def small_call(kernel, name, out_shape, args, scratch=()):
    return pl.pallas_call(
        kernel,
        in_specs=[smem_spec()] + [vmem_spec()] * (len(args) - 1),
        out_specs=[vmem_spec()] * len(out_shape),
        out_shape=out_shape,
        scratch_shapes=list(scratch),
        compiler_params=pltpu.CompilerParams(vmem_limit_bytes=VMEM_LIMIT),
        cost_estimate=BRIEF,
        name=name,
    )(*args)


def weight_kernel(at, ids_ref, x_ref, mean_ref, gb_ref, bias_ref, own_ref, *rest):
    sends, sums = rest[:3], rest[3]
    width = gb_ref.shape[1]
    grad = gb_ref[...]
    sums[:width] = jnp.dot(x_ref[...].T, grad, preferred_element_type=F32)
    sums[width : 2 * width] = jnp.dot(mean_ref[...].T, grad, preferred_element_type=F32)
    sums[2 * width :] = bias_ref[...]
    rows, extra = width // 4, bias_ref.shape[0] // 4
    for x, out in enumerate((own_ref,) + sends):
        quarter = ids_ref[at + x]
        for base, count, to in ((0, rows, 0), (width, rows, rows), (2 * width, extra, 2 * rows)):
            start = pl.multiple_of(base + quarter * count, 16)
            out[to : to + count] = sums[pl.ds(start, count)].astype(out.dtype)


def quad_sum_kernel(at, ids_ref, own_ref, one_ref, two_ref, three_ref, keep_ref, send_ref):
    total = own_ref[...] + one_ref[...].astype(F32)
    total = total + (two_ref[...].astype(F32) + three_ref[...].astype(F32))
    extra = keep_ref.shape[0] * 2 - own_ref.shape[0]
    rows = keep_ref.shape[0] - extra
    first = ids_ref[at] == 0
    keep_ref[:rows] = jnp.where(first, total[:rows], total[rows : 2 * rows])
    send_ref[:rows] = jnp.where(first, total[rows : 2 * rows], total[:rows])
    keep_ref[rows:] = total[2 * rows :]
    send_ref[rows:] = total[2 * rows :]


def join_kernel(at, ids_ref, *refs):
    parts, (matrix_ref, bias_ref) = refs[:-2], refs[-2:]
    rows, extra = matrix_ref.shape[0] // 4, bias_ref.shape[0] // 4
    for x, part in enumerate(parts):
        quarter = ids_ref[at + x]
        matrix_ref[pl.ds(pl.multiple_of(quarter * rows, 16), rows)] = part[:rows]
        bias_ref[pl.ds(pl.multiple_of(quarter * extra, 16), extra)] = part[rows:]


def scale_kernel(at, scale, ids_ref, own_ref, got_ref, bias_ref, self_ref, neigh_ref, sum_ref):
    first = ids_ref[at] == 0
    own, got = own_ref[...].astype(F32) * scale, got_ref[...].astype(F32) * scale
    self_ref[...] = jnp.where(first, own, got)
    neigh_ref[...] = jnp.where(first, got, own)
    sum_ref[...] = jnp.sum(bias_ref[...].astype(F32), axis=0, keepdims=True) * scale


def local(
    node_features, tile_rows, tile_cols, tile_masks, tile_count,
    weight_self, weight_neigh, bias_term, out_grad,
):
    node_rows, width = node_features.shape
    n = lax.axis_size("row")
    grid_cols = lax.axis_size("col")
    slots = tile_masks.shape[2]
    block_rows = grid_cols * node_rows // 128
    block_cols = n * node_rows // 128
    half = node_rows // 2
    far = n // 2

    order = ring_order(n)
    clockwise = [(order[k], order[(k + 1) % n]) for k in range(n)]
    counter = [(b, a) for a, b in clockwise]
    swap = [(0, 1), (1, 0)]
    row_id = lax.axis_index("row")
    side = lax.axis_index("col").astype(jnp.int32)
    shard_cols = node_rows // 128
    at_side, at_other, at_quad = n, n + 1, n + 2
    known = [
        [order[(order.index(r) + k) % n] * shard_cols for k in range(n)]
        + [c, 1 - c]
        + [(r & 3) ^ x for x in range(4)]
        for r in range(n)
        for c in range(grid_cols)
    ]
    ids = lax.dynamic_index_in_dim(
        jnp.array(known, jnp.int32), row_id * grid_cols + side, 0, keepdims=False
    )

    row_index = tile_rows.reshape(slots)
    col_index = tile_cols.reshape(slots)
    masks = jnp.transpose(tile_masks.reshape(slots, 128, 8), (0, 2, 1))
    slot_ids = jnp.arange(slots, dtype=jnp.int32)
    live = slot_ids < tile_count.reshape(())
    keys = jnp.where(live, col_index * block_rows + row_index, -1)
    spots = jnp.arange(block_rows * block_cols, dtype=jnp.int32)
    table = jnp.max(jnp.where(keys[None, :] == spots[:, None], slot_ids[None, :], -1), axis=1)
    counts = jnp.sum(lax.population_count(masks), axis=1).astype(BF16)
    pick = ((jnp.arange(block_rows, dtype=jnp.int32)[:, None] == row_index[None, :]) & live[None, :])
    degree = jnp.dot(pick.astype(BF16), counts, preferred_element_type=F32).reshape(2, 1, node_rows)
    sent_degree = lax.ppermute(lax.dynamic_index_in_dim(degree, 1 - side, 0, False), "col", swap)
    degree = lax.dynamic_index_in_dim(degree, side, 0, False) + sent_degree
    divisor = jnp.maximum(degree, 1.0)

    forward = partial(forward_mm, ids=ids, table=table, masks=masks, block_rows=block_rows, tblk=1024)
    row_total = block_rows * 128
    from_left = from_right = node_features
    pieces, cols, acc = [node_features], [(0, 0)], None
    early = (node_features, weight_self, bias_term, out_grad, ids, divisor)
    for s in range(1, far + 1):
        if s < far:
            next_left = lax.ppermute(from_left, "row", clockwise)
            next_right = lax.ppermute(from_right, "row", counter)
            next_cols = [(n - s, 0), (s, 0)]
        else:
            next_left = lax.ppermute(from_left[:half], "row", clockwise)
            next_right = lax.ppermute(from_right[half:], "row", counter)
        acc = forward(
            pieces, cols, None, acc=acc, out_rows=row_total, out_dtype=F32, name="forward_step"
        )
        if s == 2:
            x_now, ws_now, b_now, og_now, ids_now, div_now = early
            own_part = jnp.dot(x_now, ws_now, preferred_element_type=F32) + b_now
            far_tiles = shard_tiles(far, node_rows, ids_now, table, masks, block_rows)
            early = (own_part, og_now.astype(F32), far_tiles, div_now)
        acc, from_left, early = lax.optimization_barrier((acc, next_left, early))
        acc, from_right = lax.optimization_barrier((acc, next_right))
        pieces, cols = [from_left, from_right], next_cols
    own_part, wide_out_grad, far_tiles, divisor = early
    for_other = last_forward(pieces, at_other, ids, far_tiles, acc, BF16, "forward_send")
    received = lax.ppermute(for_other, "col", swap)
    mine = last_forward(pieces, at_side, ids, far_tiles, acc, F32, "forward_keep")
    mine, received = lax.optimization_barrier((mine, received))

    mean, node_out, grad_b, mean_grad, bias_part = middle(
        mine, received, divisor, own_part, wide_out_grad, weight_neigh
    )
    other_grad = lax.ppermute(mean_grad, "col", swap)

    backward = partial(
        backward_mm, ids=ids, table=table, masks=masks, piece_rows=node_rows, block_rows=block_rows
    )
    far_terms = first_backward(mean_grad, at_side, ids, far_tiles, None, F32, "backward_far_own")
    far_terms = first_backward(other_grad, at_other, ids, far_tiles, far_terms, BF16, "backward_far")
    both_grads, both_sides = [mean_grad, other_grad], [at_side, at_other]

    grad_scale = (node_rows * n * grid_cols) ** (-0.5)
    bits = int(math.log2(n))

    def array(rows, dtype):
        return jax.ShapeDtypeStruct((rows, width), dtype)

    def to_quad(parts, axis="row"):
        return [lax.ppermute(part, axis, [(r, r ^ x) for r in range(n)]) for x, part in parts]

    def start_quad(parts):
        quarter = 2 * (width // 4) + 16
        own, *sends = small_call(
            partial(weight_kernel, at_quad), "weight_grads",
            [array(quarter, F32)] + [array(quarter, BF16)] * 3, (ids,) + parts,
            scratch=[pltpu.VMEM((2 * width + 64, width), F32)],
        )
        return [own] + to_quad(list(enumerate(sends, 1)))

    def to_core(parts):
        keep, send = small_call(
            partial(quad_sum_kernel, at_side), "quad_sums", [array(width // 4 + 16, F32)] * 2,
            (ids,) + tuple(parts),
        )
        return [keep, lax.ppermute(send, "col", swap)]

    def add_all(b, parts):
        quarter = parts[0] + parts[1]
        return [quarter, lax.ppermute(quarter, "row", [(r, r ^ (1 << b)) for r in range(n)])]

    def from_quad(parts):
        quarter = (parts[0] + parts[1]).astype(BF16)
        return [quarter] + to_quad([(x, quarter) for x in (1, 2, 3)])

    spread = [[] for _ in range(far)]
    spread[0].append(start_quad)
    spread[1].append(to_core)
    for b in range(2, bits):
        spread[b - 1].append(partial(add_all, b))
    spread[bits - 1].append(from_quad)

    weights = (node_features, mean, grad_b, bias_part)
    right, left = far_terms[:half], far_terms[half:]
    for s in range(far - 1, -1, -1):
        mean_grad, other_grad = both_grads
        right, mean_grad = lax.optimization_barrier((right, mean_grad))
        left, other_grad = lax.optimization_barrier((left, other_grad))
        grads = [mean_grad, other_grad]
        right = lax.ppermute(right, "row", clockwise)
        left = lax.ppermute(left, "row", counter)
        if s > 0:
            terms = backward(
                [s, n - s], grads, both_sides, grads[0], acc=None, out_dtype=BF16, name="backward_step"
            )
        else:
            terms = backward(
                [0], grads, both_sides, grads[0], acc=None, out_dtype=F32, name="backward_own"
            )
            self_term = lax.dot_general(
                grad_b, weight_self, (((1,), (1,)), ((), ())), preferred_element_type=F32
            )
            terms = terms + self_term
        terms, weights = lax.optimization_barrier((terms, weights))
        for one in spread[far - 1 - s]:
            weights = one(weights)
        terms, both_grads = lax.optimization_barrier((terms, grads))
        if s > 0:
            if s == far - 1:
                gap = jnp.zeros((half, width), BF16)
                right = jnp.concatenate([right, gap], axis=0)
                left = jnp.concatenate([gap, left], axis=0)
            right = (terms[:node_rows].astype(F32) + right.astype(F32)).astype(BF16)
            left = (terms[node_rows:].astype(F32) + left.astype(F32)).astype(BF16)
        else:
            feature_grad = (terms + right.astype(F32) + left.astype(F32)).astype(BF16)

    matrix, bias_sums = small_call(
        partial(join_kernel, at_quad), "join_grads", [array(width, BF16), array(64, BF16)],
        (ids,) + tuple(weights),
    )
    got = lax.ppermute(matrix, "col", swap)
    grad_self, grad_neigh, grad_bias = small_call(
        partial(scale_kernel, at_side, grad_scale), "scale_grads",
        [array(width, F32)] * 2 + [array(1, F32)], (ids, matrix, got, bias_sums),
    )
    grad_bias = grad_bias.reshape(width)
    return node_out, feature_grad, grad_self, grad_neigh, grad_bias


def solution(mesh):
    in_specs = (
        P(("groups", "row", "col"), None),
        P(("groups", "row"), "col", None),
        P(("groups", "row"), "col", None),
        P(("groups", "row"), "col", None, None, None),
        P(("groups", "row"), "col"),
        P(),
        P(),
        P(),
        P(("groups", "row", "col"), None),
    )
    out_specs = (
        P(("groups", "row", "col"), None),
        P(("groups", "row", "col"), None),
        P("groups", None),
        P("groups", None),
        P("groups"),
    )
    return jax.shard_map(local, mesh=mesh, in_specs=in_specs, out_specs=out_specs, check_vma=False)
```

```python
from functools import partial
import math

import jax
import jax.numpy as jnp
from jax import lax
from jax.experimental import pallas as pl
from jax.experimental.pallas import tpu as pltpu
from jax.sharding import PartitionSpec as P

VMEM_LIMIT = 20 * 1024 * 1024
LAYER_BLOCK = 1024
BRIEF = pl.CostEstimate(flops=1024, bytes_accessed=1024, transcendentals=0)
GELU_C = math.sqrt(2.0 / math.pi)
F32 = jnp.float32
BF16 = jnp.bfloat16


def ring_order(n):
    return list(range(0, n, 2)) + list(range(n - 1, 0, -2))


def unpack_tile(masks_ref, slot, test):
    words = masks_ref[jnp.maximum(slot, 0)]
    words = jnp.where(slot >= 0, words, 0)
    one, zero = jnp.ones((), BF16), jnp.zeros((), BF16)
    parts = []
    for k in range(8):
        row = jnp.broadcast_to(words[k : k + 1, :], (16, 128)).astype(jnp.int16)
        parts.append(jnp.where(jnp.bitwise_and(row, test) != 0, one, zero))
    return jnp.concatenate(parts, axis=0)


def bit_tests():
    return jnp.left_shift(jnp.ones((), jnp.int16), lax.broadcasted_iota(jnp.int16, (16, 128), 0))


def fill_tiles(table_ref, masks_ref, block_rows, first_col, cols, row_of, tiles, dst):
    test = bit_tests()

    for c in range(cols):
        base = (first_col + c) * block_rows
        for r in range(tiles):
            tile = unpack_tile(masks_ref, table_ref[base + row_of(r)], test)
            dst[128 * c : 128 * c + 128, 128 * r : 128 * r + 128] = tile


def vmem_spec():
    return pl.BlockSpec(memory_space=pltpu.VMEM)


def smem_spec():
    return pl.BlockSpec(memory_space=pltpu.SMEM)


def forward_kernel(cols, side_at, block_rows, tblk, has_acc, ids_ref, table_ref, masks_ref, *refs):
    count = len(cols)
    xs = refs[:count]
    acc_ref = refs[count] if has_acc else None
    out_ref, turned, tiles = refs[count + int(has_acc) :]
    rows = xs[0].shape[0]
    for k in range(count):
        turned[:, k * rows : (k + 1) * rows] = xs[k][...].T
    first = ids_ref[side_at] * out_ref.shape[1] if side_at is not None else 0

    def block(q, carry):
        start = pl.multiple_of(q * tblk, tblk)
        begin = first + start
        first_row = begin // 128
        for k in range(count):
            at, extra = cols[k]
            fill_tiles(
                table_ref, masks_ref, block_rows, ids_ref[at] + extra, rows // 128,
                lambda r: first_row + r, tblk // 128, tiles.at[pl.ds(k * rows, rows)],
            )
        total = jnp.dot(turned[...], tiles[...], preferred_element_type=F32)
        if has_acc:
            total = total + acc_ref[:, pl.ds(pl.multiple_of(begin, tblk), tblk)]
        out_ref[:, pl.ds(start, tblk)] = total.astype(out_ref.dtype)
        return carry

    lax.fori_loop(0, out_ref.shape[1] // tblk, block, 0)


def forward_mm(pieces, cols, side_at, ids, table, masks, acc, out_rows, tblk, block_rows, out_dtype, name):
    rows, width = pieces[0].shape
    count = len(pieces)
    args = [ids, table, masks] + list(pieces) + ([] if acc is None else [acc])
    return pl.pallas_call(
        partial(forward_kernel, tuple(cols), side_at, block_rows, tblk, acc is not None),
        in_specs=[smem_spec(), smem_spec()] + [vmem_spec()] * (len(args) - 2),
        out_specs=vmem_spec(),
        scratch_shapes=[
            pltpu.VMEM((width, count * rows), BF16),
            pltpu.VMEM((count * rows, tblk), BF16),
        ],
        out_shape=jax.ShapeDtypeStruct((width, out_rows), out_dtype),
        compiler_params=pltpu.CompilerParams(vmem_limit_bytes=VMEM_LIMIT),
        cost_estimate=BRIEF,
        name=name,
    )(*args)


def shard_kernel(at, block_rows, ids_ref, table_ref, masks_ref, out_ref):
    fill_tiles(
        table_ref, masks_ref, block_rows, ids_ref[at], out_ref.shape[0] // 128,
        lambda r: r, block_rows, out_ref,
    )


def shard_tiles(at, node_rows, ids, table, masks, block_rows):
    return pl.pallas_call(
        partial(shard_kernel, at, block_rows),
        in_specs=[smem_spec(), smem_spec(), vmem_spec()],
        out_specs=vmem_spec(),
        out_shape=jax.ShapeDtypeStruct((node_rows, block_rows * 128), BF16),
        compiler_params=pltpu.CompilerParams(vmem_limit_bytes=VMEM_LIMIT),
        cost_estimate=BRIEF,
        name="far_tiles",
    )(ids, table, masks)


def last_kernel(at, ids_ref, tiles_ref, low_ref, high_ref, acc_ref, out_ref, turned):
    half = low_ref.shape[0]
    turned[:, :half] = low_ref[...].T
    turned[:, half:] = high_ref[...].T
    rows = out_ref.shape[1]
    columns = pl.ds(pl.multiple_of(ids_ref[at] * rows, rows), rows)
    total = jnp.dot(turned[...], tiles_ref[:, columns], preferred_element_type=F32)
    out_ref[...] = (total + acc_ref[:, columns]).astype(out_ref.dtype)


def last_forward(pieces, at, ids, tiles, acc, out_dtype, name):
    half, width = pieces[0].shape
    rows = acc.shape[1] // 2
    return pl.pallas_call(
        partial(last_kernel, at),
        in_specs=[smem_spec()] + [vmem_spec()] * 4,
        out_specs=vmem_spec(),
        out_shape=jax.ShapeDtypeStruct((width, rows), out_dtype),
        scratch_shapes=[pltpu.VMEM((width, 2 * half), BF16)],
        compiler_params=pltpu.CompilerParams(vmem_limit_bytes=VMEM_LIMIT),
        cost_estimate=BRIEF,
        name=name,
    )(ids, tiles, *pieces, acc)


def first_kernel(at, has_acc, ids_ref, tiles_ref, grad_ref, *refs):
    out_ref = refs[-1]
    rows = grad_ref.shape[0]
    columns = pl.ds(pl.multiple_of(ids_ref[at] * rows, rows), rows)
    total = jnp.dot(tiles_ref[:, columns], grad_ref[...], preferred_element_type=F32)
    if has_acc:
        total = total + refs[0][...]
    out_ref[...] = total.astype(out_ref.dtype)


def first_backward(grad, at, ids, tiles, acc, out_dtype, name):
    rows, width = grad.shape
    args = [ids, tiles, grad] + ([] if acc is None else [acc])
    return pl.pallas_call(
        partial(first_kernel, at, acc is not None),
        in_specs=[smem_spec()] + [vmem_spec()] * (len(args) - 1),
        out_specs=vmem_spec(),
        out_shape=jax.ShapeDtypeStruct((tiles.shape[0], width), out_dtype),
        compiler_params=pltpu.CompilerParams(vmem_limit_bytes=VMEM_LIMIT),
        cost_estimate=BRIEF,
        name=name,
    )(*args)


def middle_kernel(
    blk, agg_ref, other_ref, div_ref, own_ref, og_ref, wn_ref,
    mean_ref, out_ref, gb_ref, mg_ref, bias_ref,
):
    rows, width = own_ref.shape
    bias_ref[...] = jnp.zeros_like(bias_ref)

    def block(i, carry):
        here = pl.ds(pl.multiple_of(i * blk, blk), blk)
        div = div_ref[:, here]
        mean = ((agg_ref[:, here] + other_ref[:, here].astype(F32)) / div).T.astype(BF16)
        mean_ref[here] = mean
        pre = own_ref[here] + jnp.dot(mean, wn_ref[...], preferred_element_type=F32)
        square = pre * pre
        bent = jnp.tanh(GELU_C * (pre + 0.044715 * (square * pre)))
        half = 0.5 * (1.0 + bent)
        out_ref[here] = (pre * half).astype(BF16)
        slope = half + 0.5 * pre * (1.0 - bent * bent) * (GELU_C * (1.0 + 3.0 * 0.044715 * square))
        pre_grad = og_ref[here] * slope
        grad_b = pre_grad.astype(BF16)
        gb_ref[here] = grad_b
        div_column = jnp.broadcast_to(div, (128, blk)).T
        div_full = jnp.concatenate([div_column] * (width // 128), axis=1)
        mean_grad = lax.dot_general(
            grad_b, wn_ref[...], (((1,), (1,)), ((), ())), preferred_element_type=F32
        )
        mg_ref[here] = (mean_grad / div_full).astype(BF16)
        bias_ref[...] += jnp.sum(pre_grad.reshape(blk // 64, 64, width), axis=0)
        return carry

    lax.fori_loop(0, rows // blk, block, 0)


def middle(agg, other, divisor, own, og, wn, blk=LAYER_BLOCK):
    rows, width = own.shape
    act = jax.ShapeDtypeStruct((rows, width), BF16)
    return pl.pallas_call(
        partial(middle_kernel, blk),
        in_specs=[vmem_spec()] * 6,
        out_specs=[vmem_spec()] * 5,
        out_shape=[act] * 4 + [jax.ShapeDtypeStruct((64, width), F32)],
        compiler_params=pltpu.CompilerParams(vmem_limit_bytes=VMEM_LIMIT),
        cost_estimate=BRIEF,
        name="layer",
    )(agg, other, divisor, own, og, wn)


def backward_kernel(cols, sides, block_rows, has_acc, ids_ref, table_ref, masks_ref, after_ref, *refs):
    del after_ref
    grads = refs[: len(sides)]
    acc_ref = refs[len(sides)] if has_acc else None
    out_ref, tiles = refs[len(sides) + int(has_acc) :]
    piece_rows = out_ref.shape[0]
    rows = grads[0].shape[0]
    per_side = rows // 128
    first_col = ids_ref[cols[0]]
    for p in range(1, len(cols)):
        first_col = jnp.where(pl.program_id(0) == p, ids_ref[cols[p]], first_col)
    for k, side_at in enumerate(sides):
        base = ids_ref[side_at] * per_side
        fill_tiles(
            table_ref, masks_ref, block_rows, first_col, piece_rows // 128,
            lambda r: base + r, per_side, tiles.at[:, pl.ds(k * rows, rows)],
        )
    total = None
    for k in range(len(sides)):
        term = jnp.dot(
            tiles[:, k * rows : (k + 1) * rows], grads[k][...], preferred_element_type=F32
        )
        total = term if total is None else total + term
    if has_acc:
        total = total + acc_ref[...].astype(F32)
    out_ref[...] = total.astype(out_ref.dtype)


def backward_mm(cols, grads, sides, after, ids, table, masks, acc, piece_rows, block_rows, out_dtype, name):
    rows, width = grads[0].shape
    args = [ids, table, masks, after] + list(grads) + ([] if acc is None else [acc])
    piece = pl.BlockSpec((piece_rows, width), lambda p: (p, 0))
    return pl.pallas_call(
        partial(backward_kernel, tuple(cols), tuple(sides), block_rows, acc is not None),
        grid=(len(cols),),
        in_specs=[smem_spec(), smem_spec(), vmem_spec(), pl.BlockSpec(memory_space=pl.ANY)]
        + [vmem_spec()] * len(grads)
        + ([] if acc is None else [piece]),
        out_specs=piece,
        scratch_shapes=[pltpu.VMEM((piece_rows, len(grads) * rows), BF16)],
        out_shape=jax.ShapeDtypeStruct((len(cols) * piece_rows, width), out_dtype),
        compiler_params=pltpu.CompilerParams(vmem_limit_bytes=VMEM_LIMIT),
        cost_estimate=pl.CostEstimate(
            flops=8 * len(cols) * piece_rows * rows * len(grads) * width,
            bytes_accessed=masks.size * 4 + 4 * len(cols) * piece_rows * width,
            transcendentals=0,
        ),
        name=name,
    )(*args)


def small_call(kernel, name, out_shape, args, scratch=()):
    return pl.pallas_call(
        kernel,
        in_specs=[smem_spec()] + [vmem_spec()] * (len(args) - 1),
        out_specs=[vmem_spec()] * len(out_shape),
        out_shape=out_shape,
        scratch_shapes=list(scratch),
        compiler_params=pltpu.CompilerParams(vmem_limit_bytes=VMEM_LIMIT),
        cost_estimate=BRIEF,
        name=name,
    )(*args)


def weight_kernel(at, ids_ref, x_ref, mean_ref, gb_ref, bias_ref, own_ref, *rest):
    sends, sums = rest[:3], rest[3]
    width = gb_ref.shape[1]
    grad = gb_ref[...]
    sums[:width] = jnp.dot(x_ref[...].T, grad, preferred_element_type=F32)
    sums[width : 2 * width] = jnp.dot(mean_ref[...].T, grad, preferred_element_type=F32)
    sums[2 * width :] = bias_ref[...]
    rows, extra = width // 4, bias_ref.shape[0] // 4
    for x, out in enumerate((own_ref,) + sends):
        quarter = ids_ref[at + x]
        for base, count, to in ((0, rows, 0), (width, rows, rows), (2 * width, extra, 2 * rows)):
            start = pl.multiple_of(base + quarter * count, 16)
            out[to : to + count] = sums[pl.ds(start, count)].astype(out.dtype)


def quad_sum_kernel(at, ids_ref, own_ref, one_ref, two_ref, three_ref, keep_ref, send_ref):
    total = own_ref[...] + one_ref[...].astype(F32)
    total = total + (two_ref[...].astype(F32) + three_ref[...].astype(F32))
    extra = keep_ref.shape[0] * 2 - own_ref.shape[0]
    rows = keep_ref.shape[0] - extra
    first = ids_ref[at] == 0
    keep_ref[:rows] = jnp.where(first, total[:rows], total[rows : 2 * rows])
    send_ref[:rows] = jnp.where(first, total[rows : 2 * rows], total[:rows])
    keep_ref[rows:] = total[2 * rows :]
    send_ref[rows:] = total[2 * rows :]


def join_kernel(at, ids_ref, *refs):
    parts, (matrix_ref, bias_ref) = refs[:-2], refs[-2:]
    rows, extra = matrix_ref.shape[0] // 4, bias_ref.shape[0] // 4
    for x, part in enumerate(parts):
        quarter = ids_ref[at + x]
        matrix_ref[pl.ds(pl.multiple_of(quarter * rows, 16), rows)] = part[:rows]
        bias_ref[pl.ds(pl.multiple_of(quarter * extra, 16), extra)] = part[rows:]


def scale_kernel(at, scale, ids_ref, own_ref, got_ref, bias_ref, self_ref, neigh_ref, sum_ref):
    first = ids_ref[at] == 0
    own, got = own_ref[...].astype(F32) * scale, got_ref[...].astype(F32) * scale
    self_ref[...] = jnp.where(first, own, got)
    neigh_ref[...] = jnp.where(first, got, own)
    sum_ref[...] = jnp.sum(bias_ref[...].astype(F32), axis=0, keepdims=True) * scale


def local(
    node_features, tile_rows, tile_cols, tile_masks, tile_count,
    weight_self, weight_neigh, bias_term, out_grad,
):
    node_rows, width = node_features.shape
    n = lax.axis_size("row")
    grid_cols = lax.axis_size("col")
    slots = tile_masks.shape[2]
    block_rows = grid_cols * node_rows // 128
    block_cols = n * node_rows // 128
    half = node_rows // 2
    far = n // 2

    order = ring_order(n)
    clockwise = [(order[k], order[(k + 1) % n]) for k in range(n)]
    counter = [(b, a) for a, b in clockwise]
    swap = [(0, 1), (1, 0)]
    row_id = lax.axis_index("row")
    side = lax.axis_index("col").astype(jnp.int32)
    shard_cols = node_rows // 128
    at_side, at_other, at_quad = n, n + 1, n + 2
    known = [
        [order[(order.index(r) + k) % n] * shard_cols for k in range(n)]
        + [c, 1 - c]
        + [(r & 3) ^ x for x in range(4)]
        for r in range(n)
        for c in range(grid_cols)
    ]
    ids = lax.dynamic_index_in_dim(
        jnp.array(known, jnp.int32), row_id * grid_cols + side, 0, keepdims=False
    )

    row_index = tile_rows.reshape(slots)
    col_index = tile_cols.reshape(slots)
    masks = jnp.transpose(tile_masks.reshape(slots, 128, 8), (0, 2, 1))
    slot_ids = jnp.arange(slots, dtype=jnp.int32)
    live = slot_ids < tile_count.reshape(())
    keys = jnp.where(live, col_index * block_rows + row_index, -1)
    spots = jnp.arange(block_rows * block_cols, dtype=jnp.int32)
    table = jnp.max(jnp.where(keys[None, :] == spots[:, None], slot_ids[None, :], -1), axis=1)
    counts = jnp.sum(lax.population_count(masks), axis=1).astype(BF16)
    pick = ((jnp.arange(block_rows, dtype=jnp.int32)[:, None] == row_index[None, :]) & live[None, :])
    degree = jnp.dot(pick.astype(BF16), counts, preferred_element_type=F32).reshape(2, 1, node_rows)
    sent_degree = lax.ppermute(lax.dynamic_index_in_dim(degree, 1 - side, 0, False), "col", swap)
    degree = lax.dynamic_index_in_dim(degree, side, 0, False) + sent_degree
    divisor = jnp.maximum(degree, 1.0)

    row_total = block_rows * 128
    forward = partial(forward_mm, ids=ids, table=table, masks=masks, block_rows=block_rows, tblk=row_total)
    from_left = from_right = node_features
    pieces, cols, acc = [node_features], [(0, 0)], None
    early = (node_features, weight_self, bias_term, out_grad, ids, divisor)
    for s in range(1, far + 1):
        if s < far:
            next_left = lax.ppermute(from_left, "row", clockwise)
            next_right = lax.ppermute(from_right, "row", counter)
            next_cols = [(n - s, 0), (s, 0)]
        else:
            next_left = lax.ppermute(from_left[:half], "row", clockwise)
            next_right = lax.ppermute(from_right[half:], "row", counter)
        acc = forward(
            pieces, cols, None, acc=acc, out_rows=row_total, out_dtype=F32, name="forward_step"
        )
        if s == 2:
            x_now, ws_now, b_now, og_now, ids_now, div_now = early
            own_part = jnp.dot(x_now, ws_now, preferred_element_type=F32) + b_now
            far_tiles = shard_tiles(far, node_rows, ids_now, table, masks, block_rows)
            early = (own_part, og_now.astype(F32), far_tiles, div_now)
        acc, from_left, early = lax.optimization_barrier((acc, next_left, early))
        acc, from_right = lax.optimization_barrier((acc, next_right))
        pieces, cols = [from_left, from_right], next_cols
    own_part, wide_out_grad, far_tiles, divisor = early
    for_other = last_forward(pieces, at_other, ids, far_tiles, acc, BF16, "forward_send")
    received = lax.ppermute(for_other, "col", swap)
    mine = last_forward(pieces, at_side, ids, far_tiles, acc, F32, "forward_keep")
    mine, received = lax.optimization_barrier((mine, received))

    mean, node_out, grad_b, mean_grad, bias_part = middle(
        mine, received, divisor, own_part, wide_out_grad, weight_neigh
    )
    other_grad = lax.ppermute(mean_grad, "col", swap)

    backward = partial(
        backward_mm, ids=ids, table=table, masks=masks, piece_rows=node_rows, block_rows=block_rows
    )
    far_terms = first_backward(mean_grad, at_side, ids, far_tiles, None, F32, "backward_far_own")
    far_terms = first_backward(other_grad, at_other, ids, far_tiles, far_terms, BF16, "backward_far")
    both_grads, both_sides = [mean_grad, other_grad], [at_side, at_other]

    grad_scale = (node_rows * n * grid_cols) ** (-0.5)
    bits = int(math.log2(n))

    def array(rows, dtype):
        return jax.ShapeDtypeStruct((rows, width), dtype)

    def to_quad(parts, axis="row"):
        return [lax.ppermute(part, axis, [(r, r ^ x) for r in range(n)]) for x, part in parts]

    def start_quad(parts):
        quarter = 2 * (width // 4) + 16
        own, *sends = small_call(
            partial(weight_kernel, at_quad), "weight_grads",
            [array(quarter, F32)] + [array(quarter, BF16)] * 3, (ids,) + parts,
            scratch=[pltpu.VMEM((2 * width + 64, width), F32)],
        )
        return [own] + to_quad(list(enumerate(sends, 1)))

    def to_core(parts):
        keep, send = small_call(
            partial(quad_sum_kernel, at_side), "quad_sums", [array(width // 4 + 16, F32)] * 2,
            (ids,) + tuple(parts),
        )
        return [keep, lax.ppermute(send, "col", swap)]

    def add_all(b, parts):
        quarter = (parts[0].astype(F32) + parts[1].astype(F32)).astype(BF16)
        return [quarter, lax.ppermute(quarter, "row", [(r, r ^ (1 << b)) for r in range(n)])]

    def from_quad(parts):
        quarter = (parts[0].astype(F32) + parts[1].astype(F32)).astype(BF16)
        return [quarter] + to_quad([(x, quarter) for x in (1, 2, 3)])

    spread = [[] for _ in range(far)]
    spread[0].append(start_quad)
    spread[1].append(to_core)
    for b in range(2, bits):
        spread[b - 1].append(partial(add_all, b))
    spread[bits - 1].append(from_quad)

    weights = (node_features, mean, grad_b, bias_part)
    right, left = far_terms[:half], far_terms[half:]
    for s in range(far - 1, -1, -1):
        mean_grad, other_grad = both_grads
        right, mean_grad = lax.optimization_barrier((right, mean_grad))
        left, other_grad = lax.optimization_barrier((left, other_grad))
        grads = [mean_grad, other_grad]
        right = lax.ppermute(right, "row", clockwise)
        left = lax.ppermute(left, "row", counter)
        if s > 0:
            terms = backward(
                [s, n - s], grads, both_sides, grads[0], acc=None, out_dtype=BF16, name="backward_step"
            )
        else:
            terms = backward(
                [0], grads, both_sides, grads[0], acc=None, out_dtype=F32, name="backward_own"
            )
            self_term = lax.dot_general(
                grad_b, weight_self, (((1,), (1,)), ((), ())), preferred_element_type=F32
            )
            terms = terms + self_term
        terms, weights = lax.optimization_barrier((terms, weights))
        for one in spread[far - 1 - s]:
            weights = one(weights)
        terms, both_grads = lax.optimization_barrier((terms, grads))
        if s > 0:
            if s == far - 1:
                gap = jnp.zeros((half, width), BF16)
                right = jnp.concatenate([right, gap], axis=0)
                left = jnp.concatenate([gap, left], axis=0)
            right = (terms[:node_rows].astype(F32) + right.astype(F32)).astype(BF16)
            left = (terms[node_rows:].astype(F32) + left.astype(F32)).astype(BF16)
        else:
            feature_grad = (terms + right.astype(F32) + left.astype(F32)).astype(BF16)

    matrix, bias_sums = small_call(
        partial(join_kernel, at_quad), "join_grads", [array(width, BF16), array(64, BF16)],
        (ids,) + tuple(weights),
    )
    got = lax.ppermute(matrix, "col", swap)
    grad_self, grad_neigh, grad_bias = small_call(
        partial(scale_kernel, at_side, grad_scale), "scale_grads",
        [array(width, F32)] * 2 + [array(1, F32)], (ids, matrix, got, bias_sums),
    )
    grad_bias = grad_bias.reshape(width)
    return node_out, feature_grad, grad_self, grad_neigh, grad_bias


def solution(mesh):
    in_specs = (
        P(("groups", "row", "col"), None),
        P(("groups", "row"), "col", None),
        P(("groups", "row"), "col", None),
        P(("groups", "row"), "col", None, None, None),
        P(("groups", "row"), "col"),
        P(),
        P(),
        P(),
        P(("groups", "row", "col"), None),
    )
    out_specs = (
        P(("groups", "row", "col"), None),
        P(("groups", "row", "col"), None),
        P("groups", None),
        P("groups", None),
        P("groups"),
    )
    return jax.shard_map(local, mesh=mesh, in_specs=in_specs, out_specs=out_specs, check_vma=False)
```

```python
from functools import partial
import math

import jax
import jax.numpy as jnp
from jax import lax
from jax.experimental import pallas as pl
from jax.experimental.pallas import tpu as pltpu
from jax.sharding import PartitionSpec as P

VMEM_LIMIT = 14 * 1024 * 1024
BRIEF = pl.CostEstimate(flops=1024, bytes_accessed=1024, transcendentals=0)
GELU_C = math.sqrt(2.0 / math.pi)
F32 = jnp.float32
BF16 = jnp.bfloat16


def ring_order(n):
    return list(range(0, n, 2)) + list(range(n - 1, 0, -2))


def unpack_tile(masks_ref, slot, test):
    words = masks_ref[jnp.maximum(slot, 0)]
    words = jnp.where(slot >= 0, words, 0)
    one, zero = jnp.ones((), BF16), jnp.zeros((), BF16)
    parts = []
    for k in range(8):
        row = jnp.broadcast_to(words[k : k + 1, :], (16, 128)).astype(jnp.int16)
        parts.append(jnp.where(jnp.bitwise_and(row, test) != 0, one, zero))
    return jnp.concatenate(parts, axis=0)


def bit_tests():
    return jnp.left_shift(jnp.ones((), jnp.int16), lax.broadcasted_iota(jnp.int16, (16, 128), 0))


def fill_tiles(table_ref, masks_ref, block_rows, first_col, cols, row_of, tiles, dst):
    test = bit_tests()

    for c in range(cols):
        base = (first_col + c) * block_rows
        for r in range(tiles):
            tile = unpack_tile(masks_ref, table_ref[base + row_of(r)], test)
            dst[128 * c : 128 * c + 128, 128 * r : 128 * r + 128] = tile


def vmem_spec():
    return pl.BlockSpec(memory_space=pltpu.VMEM)


def smem_spec():
    return pl.BlockSpec(memory_space=pltpu.SMEM)


def forward_kernel(cols, side_at, block_rows, tblk, has_acc, ids_ref, table_ref, masks_ref, *refs):
    count = len(cols)
    xs = refs[:count]
    acc_ref = refs[count] if has_acc else None
    out_ref, turned, tiles = refs[count + int(has_acc) :]
    rows = xs[0].shape[0]
    for k in range(count):
        turned[:, k * rows : (k + 1) * rows] = xs[k][...].T
    first = ids_ref[side_at] * out_ref.shape[1] if side_at is not None else 0

    def block(q, carry):
        start = pl.multiple_of(q * tblk, tblk)
        begin = first + start
        first_row = begin // 128
        for k in range(count):
            at, extra = cols[k]
            fill_tiles(
                table_ref, masks_ref, block_rows, ids_ref[at] + extra, rows // 128,
                lambda r: first_row + r, tblk // 128, tiles.at[pl.ds(k * rows, rows)],
            )
        total = jnp.dot(turned[...], tiles[...], preferred_element_type=F32)
        if has_acc:
            total = total + acc_ref[:, pl.ds(pl.multiple_of(begin, tblk), tblk)]
        out_ref[:, pl.ds(start, tblk)] = total.astype(out_ref.dtype)
        return carry

    lax.fori_loop(0, out_ref.shape[1] // tblk, block, 0)


def forward_mm(pieces, cols, side_at, ids, table, masks, acc, out_rows, tblk, block_rows, out_dtype, name):
    rows, width = pieces[0].shape
    count = len(pieces)
    args = [ids, table, masks] + list(pieces) + ([] if acc is None else [acc])
    turned = (width, count * rows)
    out_shape = [jax.ShapeDtypeStruct((width, out_rows), out_dtype)]
    scratch = [pltpu.VMEM((count * rows, tblk), BF16)]
    if acc is None:
        out_shape.append(jax.ShapeDtypeStruct(turned, BF16))
    else:
        scratch.insert(0, pltpu.VMEM(turned, BF16))
    return pl.pallas_call(
        partial(forward_kernel, tuple(cols), side_at, block_rows, tblk, acc is not None),
        in_specs=[smem_spec(), smem_spec()] + [vmem_spec()] * (len(args) - 2),
        out_specs=[vmem_spec()] * len(out_shape),
        scratch_shapes=scratch,
        out_shape=out_shape,
        compiler_params=pltpu.CompilerParams(vmem_limit_bytes=VMEM_LIMIT),
        cost_estimate=BRIEF,
        name=name,
    )(*args)


def shard_kernel(at, block_rows, ids_ref, table_ref, masks_ref, out_ref):
    fill_tiles(
        table_ref, masks_ref, block_rows, ids_ref[at], out_ref.shape[0] // 128,
        lambda r: r, block_rows, out_ref,
    )


def shard_tiles(at, node_rows, ids, table, masks, block_rows):
    return pl.pallas_call(
        partial(shard_kernel, at, block_rows),
        in_specs=[smem_spec(), smem_spec(), vmem_spec()],
        out_specs=vmem_spec(),
        out_shape=jax.ShapeDtypeStruct((node_rows, block_rows * 128), BF16),
        compiler_params=pltpu.CompilerParams(vmem_limit_bytes=VMEM_LIMIT),
        cost_estimate=BRIEF,
        name="far_tiles",
    )(ids, table, masks)


def last_kernel(at, ids_ref, tiles_ref, low_ref, high_ref, acc_ref, out_ref, turned):
    half = low_ref.shape[0]
    turned[:, :half] = low_ref[...].T
    turned[:, half:] = high_ref[...].T
    rows = out_ref.shape[1]
    columns = pl.ds(pl.multiple_of(ids_ref[at] * rows, rows), rows)
    total = jnp.dot(turned[...], tiles_ref[:, columns], preferred_element_type=F32)
    out_ref[...] = (total + acc_ref[:, columns]).astype(out_ref.dtype)


def last_forward(pieces, at, ids, tiles, acc, out_dtype, name):
    half, width = pieces[0].shape
    rows = acc.shape[1] // 2
    return pl.pallas_call(
        partial(last_kernel, at),
        in_specs=[smem_spec()] + [vmem_spec()] * 4,
        out_specs=vmem_spec(),
        out_shape=jax.ShapeDtypeStruct((width, rows), out_dtype),
        scratch_shapes=[pltpu.VMEM((width, 2 * half), BF16)],
        compiler_params=pltpu.CompilerParams(vmem_limit_bytes=VMEM_LIMIT),
        cost_estimate=BRIEF,
        name=name,
    )(ids, tiles, *pieces, acc)


def first_kernel(at, has_acc, ids_ref, tiles_ref, grad_ref, *refs):
    out_ref = refs[-1]
    rows = grad_ref.shape[0]
    columns = pl.ds(pl.multiple_of(ids_ref[at] * rows, rows), rows)
    total = jnp.dot(tiles_ref[:, columns], grad_ref[...], preferred_element_type=F32)
    if has_acc:
        total = total + refs[0][...]
    out_ref[...] = total.astype(out_ref.dtype)


def first_backward(grad, at, ids, tiles, acc, out_dtype, name):
    rows, width = grad.shape
    args = [ids, tiles, grad] + ([] if acc is None else [acc])
    return pl.pallas_call(
        partial(first_kernel, at, acc is not None),
        in_specs=[smem_spec()] + [vmem_spec()] * (len(args) - 1),
        out_specs=vmem_spec(),
        out_shape=jax.ShapeDtypeStruct((tiles.shape[0], width), out_dtype),
        compiler_params=pltpu.CompilerParams(vmem_limit_bytes=VMEM_LIMIT),
        cost_estimate=BRIEF,
        name=name,
    )(*args)


def middle_kernel(
    at, ids_ref, agg_ref, other_ref, div_ref, own_ref, og_ref, wn_ref, xt_ref,
    out_ref, gb_ref, mg_ref, keep_ref, send_ref,
):
    rows, width = own_ref.shape
    div = div_ref[...]
    mean_turned = (agg_ref[...] + other_ref[...].astype(F32)) / div
    mean = mean_turned.T.astype(BF16)
    pre = own_ref[...] + jnp.dot(mean, wn_ref[...], preferred_element_type=F32)
    square = pre * pre
    bent = jnp.tanh(GELU_C * (pre + 0.044715 * (square * pre)))
    half = 0.5 * (1.0 + bent)
    out_ref[...] = (pre * half).astype(BF16)
    slope = half + 0.5 * pre * (1.0 - bent * bent) * (GELU_C * (1.0 + 3.0 * 0.044715 * square))
    pre_grad = og_ref[...] * slope
    grad_b = pre_grad.astype(BF16)
    gb_ref[...] = grad_b
    div_column = jnp.broadcast_to(div, (128, rows)).T
    div_full = jnp.concatenate([div_column] * (width // 128), axis=1)
    mean_grad = lax.dot_general(
        grad_b, wn_ref[...], (((1,), (1,)), ((), ())), preferred_element_type=F32
    )
    mg_ref[...] = (mean_grad / div_full).astype(BF16)
    own = jnp.dot(xt_ref[...], grad_b, preferred_element_type=F32)
    neigh = jnp.dot(mean_turned.astype(BF16), grad_b, preferred_element_type=F32)
    first = ids_ref[at] == 0
    keep_ref[:width] = jnp.where(first, own, neigh)
    send_ref[:width] = jnp.where(first, neigh, own)
    bias = jnp.sum(pre_grad.reshape(rows // 64, 64, width), axis=0)
    keep_ref[width:] = bias
    send_ref[width:] = bias


def middle(at, ids, agg, other, divisor, own, og, wn, x_turned):
    rows, width = own.shape
    act = jax.ShapeDtypeStruct((rows, width), BF16)
    return pl.pallas_call(
        partial(middle_kernel, at),
        in_specs=[smem_spec()] + [vmem_spec()] * 7,
        out_specs=[vmem_spec()] * 5,
        out_shape=[act] * 3 + [jax.ShapeDtypeStruct((width + 64, width), F32)] * 2,
        compiler_params=pltpu.CompilerParams(vmem_limit_bytes=VMEM_LIMIT),
        cost_estimate=BRIEF,
        name="layer",
    )(ids, agg, other, divisor, own, og, wn, x_turned)


def backward_kernel(cols, sides, block_rows, has_acc, ids_ref, table_ref, masks_ref, after_ref, *refs):
    del after_ref
    grads = refs[: len(sides)]
    acc_ref = refs[len(sides)] if has_acc else None
    out_ref, tiles = refs[len(sides) + int(has_acc) :]
    piece_rows = out_ref.shape[0]
    rows = grads[0].shape[0]
    per_side = rows // 128
    first_col = ids_ref[cols[0]]
    for p in range(1, len(cols)):
        first_col = jnp.where(pl.program_id(0) == p, ids_ref[cols[p]], first_col)
    for k, side_at in enumerate(sides):
        base = ids_ref[side_at] * per_side
        fill_tiles(
            table_ref, masks_ref, block_rows, first_col, piece_rows // 128,
            lambda r: base + r, per_side, tiles.at[:, pl.ds(k * rows, rows)],
        )
    total = None
    for k in range(len(sides)):
        term = jnp.dot(
            tiles[:, k * rows : (k + 1) * rows], grads[k][...], preferred_element_type=F32
        )
        total = term if total is None else total + term
    if has_acc:
        total = total + acc_ref[...].astype(F32)
    out_ref[...] = total.astype(out_ref.dtype)


def backward_mm(cols, grads, sides, after, ids, table, masks, acc, piece_rows, block_rows, out_dtype, name):
    rows, width = grads[0].shape
    args = [ids, table, masks, after] + list(grads) + ([] if acc is None else [acc])
    piece = pl.BlockSpec((piece_rows, width), lambda p: (p, 0))
    return pl.pallas_call(
        partial(backward_kernel, tuple(cols), tuple(sides), block_rows, acc is not None),
        grid=(len(cols),),
        in_specs=[smem_spec(), smem_spec(), vmem_spec(), pl.BlockSpec(memory_space=pl.ANY)]
        + [vmem_spec()] * len(grads)
        + ([] if acc is None else [piece]),
        out_specs=piece,
        scratch_shapes=[pltpu.VMEM((piece_rows, len(grads) * rows), BF16)],
        out_shape=jax.ShapeDtypeStruct((len(cols) * piece_rows, width), out_dtype),
        compiler_params=pltpu.CompilerParams(vmem_limit_bytes=VMEM_LIMIT),
        cost_estimate=pl.CostEstimate(
            flops=8 * len(cols) * piece_rows * rows * len(grads) * width,
            bytes_accessed=masks.size * 4 + 4 * len(cols) * piece_rows * width,
            transcendentals=0,
        ),
        name=name,
    )(*args)


def small_call(kernel, name, out_shape, args, scratch=()):
    return pl.pallas_call(
        kernel,
        in_specs=[smem_spec()] + [vmem_spec()] * (len(args) - 1),
        out_specs=[vmem_spec()] * len(out_shape),
        out_shape=out_shape,
        scratch_shapes=list(scratch),
        compiler_params=pltpu.CompilerParams(vmem_limit_bytes=VMEM_LIMIT),
        cost_estimate=BRIEF,
        name=name,
    )(*args)


def quarter_kernel(at, ids_ref, keep_ref, got_ref, own_ref, *sends):
    extra = keep_ref.shape[0] - 256 * (keep_ref.shape[0] // 256)
    rows, extra = (keep_ref.shape[0] - extra) // 4, extra // 4
    for x, out in enumerate((own_ref,) + sends):
        quarter = ids_ref[at + x]
        for base, count, to in ((0, rows, 0), (4 * rows, extra, rows)):
            here = pl.ds(pl.multiple_of(base + quarter * count, 16), count)
            out[to : to + count] = (keep_ref[here] + got_ref[here]).astype(out.dtype)


def join_kernel(at, ids_ref, *refs):
    parts, (matrix_ref, bias_ref) = refs[:-2], refs[-2:]
    rows, extra = matrix_ref.shape[0] // 4, bias_ref.shape[0] // 4
    for x, part in enumerate(parts):
        quarter = ids_ref[at + x]
        matrix_ref[pl.ds(pl.multiple_of(quarter * rows, 16), rows)] = part[:rows]
        bias_ref[pl.ds(pl.multiple_of(quarter * extra, 16), extra)] = part[rows:]


def scale_kernel(at, scale, ids_ref, own_ref, got_ref, bias_ref, self_ref, neigh_ref, sum_ref):
    first = ids_ref[at] == 0
    own, got = own_ref[...].astype(F32) * scale, got_ref[...].astype(F32) * scale
    self_ref[...] = jnp.where(first, own, got)
    neigh_ref[...] = jnp.where(first, got, own)
    sum_ref[...] = jnp.sum(bias_ref[...].astype(F32), axis=0, keepdims=True) * scale


def local(
    node_features, tile_rows, tile_cols, tile_masks, tile_count,
    weight_self, weight_neigh, bias_term, out_grad,
):
    node_rows, width = node_features.shape
    n = lax.axis_size("row")
    grid_cols = lax.axis_size("col")
    slots = tile_masks.shape[2]
    block_rows = grid_cols * node_rows // 128
    block_cols = n * node_rows // 128
    half = node_rows // 2
    far = n // 2

    order = ring_order(n)
    clockwise = [(order[k], order[(k + 1) % n]) for k in range(n)]
    counter = [(b, a) for a, b in clockwise]
    swap = [(0, 1), (1, 0)]
    row_id = lax.axis_index("row")
    side = lax.axis_index("col").astype(jnp.int32)
    shard_cols = node_rows // 128
    at_side, at_other, at_quad = n, n + 1, n + 2
    known = [
        [order[(order.index(r) + k) % n] * shard_cols for k in range(n)]
        + [c, 1 - c]
        + [(r & 3) ^ x for x in range(4)]
        for r in range(n)
        for c in range(grid_cols)
    ]
    ids = lax.dynamic_index_in_dim(
        jnp.array(known, jnp.int32), row_id * grid_cols + side, 0, keepdims=False
    )

    row_index = tile_rows.reshape(slots)
    col_index = tile_cols.reshape(slots)
    masks = jnp.transpose(tile_masks.reshape(slots, 128, 8), (0, 2, 1))
    slot_ids = jnp.arange(slots, dtype=jnp.int32)
    live = slot_ids < tile_count.reshape(())
    keys = jnp.where(live, col_index * block_rows + row_index, -1)
    spots = jnp.arange(block_rows * block_cols, dtype=jnp.int32)
    table = jnp.max(jnp.where(keys[None, :] == spots[:, None], slot_ids[None, :], -1), axis=1)
    counts = jnp.sum(lax.population_count(masks), axis=1).astype(BF16)
    pick = ((jnp.arange(block_rows, dtype=jnp.int32)[:, None] == row_index[None, :]) & live[None, :])
    degree = jnp.dot(pick.astype(BF16), counts, preferred_element_type=F32).reshape(2, 1, node_rows)
    sent_degree = lax.ppermute(lax.dynamic_index_in_dim(degree, 1 - side, 0, False), "col", swap)
    degree = lax.dynamic_index_in_dim(degree, side, 0, False) + sent_degree
    divisor = jnp.maximum(degree, 1.0)

    row_total = block_rows * 128
    forward = partial(forward_mm, ids=ids, table=table, masks=masks, block_rows=block_rows, tblk=1024)
    from_left = from_right = node_features
    pieces, cols, acc = [node_features], [(0, 0)], None
    early = (node_features, weight_self, bias_term, out_grad, ids, divisor)
    for s in range(1, far + 1):
        if s < far:
            next_left = lax.ppermute(from_left, "row", clockwise)
            next_right = lax.ppermute(from_right, "row", counter)
            next_cols = [(n - s, 0), (s, 0)]
        else:
            next_left = lax.ppermute(from_left[:half], "row", clockwise)
            next_right = lax.ppermute(from_right[half:], "row", counter)
        acc, *rest = forward(
            pieces, cols, None, acc=acc, out_rows=row_total, out_dtype=F32, name="forward_step"
        )
        x_turned = rest[0] if rest else x_turned
        if s == 2:
            x_now, ws_now, b_now, og_now, ids_now, div_now = early
            own_part = jnp.dot(x_now, ws_now, preferred_element_type=F32) + b_now
            far_tiles = shard_tiles(far, node_rows, ids_now, table, masks, block_rows)
            early = (own_part, og_now.astype(F32), far_tiles, div_now)
        acc, from_left, early = lax.optimization_barrier((acc, next_left, early))
        acc, from_right = lax.optimization_barrier((acc, next_right))
        pieces, cols = [from_left, from_right], next_cols
    own_part, wide_out_grad, far_tiles, divisor = early
    for_other = last_forward(pieces, at_other, ids, far_tiles, acc, BF16, "forward_send")
    received = lax.ppermute(for_other, "col", swap)
    mine = last_forward(pieces, at_side, ids, far_tiles, acc, F32, "forward_keep")
    mine, received = lax.optimization_barrier((mine, received))

    node_out, grad_b, mean_grad, keep, sent = middle(
        at_side, ids, mine, received, divisor, own_part, wide_out_grad, weight_neigh, x_turned
    )
    other_grad = lax.ppermute(mean_grad, "col", swap)

    backward = partial(
        backward_mm, ids=ids, table=table, masks=masks, piece_rows=node_rows, block_rows=block_rows
    )
    far_terms = first_backward(mean_grad, at_side, ids, far_tiles, None, F32, "backward_far_own")
    far_terms = first_backward(other_grad, at_other, ids, far_tiles, far_terms, BF16, "backward_far")
    both_grads, both_sides = [mean_grad, other_grad], [at_side, at_other]

    grad_scale = (node_rows * n * grid_cols) ** (-0.5)
    bits = int(math.log2(n))

    def array(rows, dtype):
        return jax.ShapeDtypeStruct((rows, width), dtype)

    def to_quad(parts, axis="row"):
        return [lax.ppermute(part, axis, [(r, r ^ x) for r in range(n)]) for x, part in parts]

    def start_quad(parts):
        own, *sends = small_call(
            partial(quarter_kernel, at_quad), "weight_quarters",
            [array(width // 4 + 16, F32)] + [array(width // 4 + 16, BF16)] * 3, (ids,) + parts,
        )
        return [own] + to_quad(list(enumerate(sends, 1)))

    def rounded_sum(parts):
        total = parts[0].astype(F32)
        for part in parts[1:]:
            total = total + part.astype(F32)
        return total.astype(BF16)

    def add_all(b, parts):
        quarter = rounded_sum(parts)
        return [quarter, lax.ppermute(quarter, "row", [(r, r ^ (1 << b)) for r in range(n)])]

    def from_quad(parts):
        quarter = rounded_sum(parts)
        return [quarter] + to_quad([(x, quarter) for x in (1, 2, 3)])

    spread = [[] for _ in range(far)]
    spread[0].append(start_quad)
    for b in range(2, bits):
        spread[b - 1].append(partial(add_all, b))
    spread[bits - 1].append(from_quad)

    weights = (keep, lax.ppermute(sent, "col", swap))
    right, left = far_terms[:half], far_terms[half:]
    for s in range(far - 1, -1, -1):
        mean_grad, other_grad = both_grads
        right, mean_grad = lax.optimization_barrier((right, mean_grad))
        left, other_grad = lax.optimization_barrier((left, other_grad))
        grads = [mean_grad, other_grad]
        right = lax.ppermute(right, "row", clockwise)
        left = lax.ppermute(left, "row", counter)
        if s > 0:
            terms = backward(
                [s, n - s], grads, both_sides, grads[0], acc=None, out_dtype=BF16, name="backward_step"
            )
        else:
            terms = backward(
                [0], grads, both_sides, grads[0], acc=None, out_dtype=F32, name="backward_own"
            )
            self_term = lax.dot_general(
                grad_b, weight_self, (((1,), (1,)), ((), ())), preferred_element_type=F32
            )
            terms = terms + self_term
        terms, weights = lax.optimization_barrier((terms, weights))
        for one in spread[far - 1 - s]:
            weights = one(weights)
        terms, both_grads = lax.optimization_barrier((terms, grads))
        if s > 0:
            if s == far - 1:
                gap = jnp.zeros((half, width), BF16)
                right = jnp.concatenate([right, gap], axis=0)
                left = jnp.concatenate([gap, left], axis=0)
            right = (terms[:node_rows].astype(F32) + right.astype(F32)).astype(BF16)
            left = (terms[node_rows:].astype(F32) + left.astype(F32)).astype(BF16)
        else:
            feature_grad = (terms + right.astype(F32) + left.astype(F32)).astype(BF16)

    matrix, bias_sums = small_call(
        partial(join_kernel, at_quad), "join_grads", [array(width, BF16), array(64, BF16)],
        (ids,) + tuple(weights),
    )
    got = lax.ppermute(matrix, "col", swap)
    grad_self, grad_neigh, grad_bias = small_call(
        partial(scale_kernel, at_side, grad_scale), "scale_grads",
        [array(width, F32)] * 2 + [array(1, F32)], (ids, matrix, got, bias_sums),
    )
    grad_bias = grad_bias.reshape(width)
    return node_out, feature_grad, grad_self, grad_neigh, grad_bias


def solution(mesh):
    in_specs = (
        P(("groups", "row", "col"), None),
        P(("groups", "row"), "col", None),
        P(("groups", "row"), "col", None),
        P(("groups", "row"), "col", None, None, None),
        P(("groups", "row"), "col"),
        P(),
        P(),
        P(),
        P(("groups", "row", "col"), None),
    )
    out_specs = (
        P(("groups", "row", "col"), None),
        P(("groups", "row", "col"), None),
        P("groups", None),
        P("groups", None),
        P("groups"),
    )
    return jax.shard_map(local, mesh=mesh, in_specs=in_specs, out_specs=out_specs, check_vma=False)
```

```python
from functools import partial
import math

import jax
import jax.numpy as jnp
from jax import lax
from jax.experimental import pallas as pl
from jax.experimental.pallas import tpu as pltpu
from jax.sharding import PartitionSpec as P

VMEM_LIMIT = 14 * 1024 * 1024
BRIEF = pl.CostEstimate(flops=1024, bytes_accessed=1024, transcendentals=0)
GELU_C = math.sqrt(2.0 / math.pi)
F32 = jnp.float32
BF16 = jnp.bfloat16


def ring_order(n):
    return list(range(0, n, 2)) + list(range(n - 1, 0, -2))


def unpack_tile(masks_ref, slot, test):
    words = masks_ref[jnp.maximum(slot, 0)]
    words = jnp.where(slot >= 0, words, 0)
    one, zero = jnp.ones((), BF16), jnp.zeros((), BF16)
    parts = []
    for k in range(8):
        row = jnp.broadcast_to(words[k : k + 1, :], (16, 128)).astype(jnp.int16)
        parts.append(jnp.where(jnp.bitwise_and(row, test) != 0, one, zero))
    return jnp.concatenate(parts, axis=0)


def bit_tests():
    return jnp.left_shift(jnp.ones((), jnp.int16), lax.broadcasted_iota(jnp.int16, (16, 128), 0))


def fill_tiles(table_ref, masks_ref, block_rows, first_col, cols, row_of, tiles, dst):
    test = bit_tests()

    for c in range(cols):
        base = (first_col + c) * block_rows
        for r in range(tiles):
            tile = unpack_tile(masks_ref, table_ref[base + row_of(r)], test)
            dst[128 * c : 128 * c + 128, 128 * r : 128 * r + 128] = tile


def vmem_spec():
    return pl.BlockSpec(memory_space=pltpu.VMEM)


def smem_spec():
    return pl.BlockSpec(memory_space=pltpu.SMEM)


def forward_kernel(cols, side_at, block_rows, tblk, has_acc, ids_ref, table_ref, masks_ref, *refs):
    count = len(cols)
    xs = refs[:count]
    acc_ref = refs[count] if has_acc else None
    out_ref, turned, tiles = refs[count + int(has_acc) :]
    rows = xs[0].shape[0]
    for k in range(count):
        turned[:, k * rows : (k + 1) * rows] = xs[k][...].T
    first = ids_ref[side_at] * out_ref.shape[1] if side_at is not None else 0

    def block(q, carry):
        start = pl.multiple_of(q * tblk, tblk)
        begin = first + start
        first_row = begin // 128
        for k in range(count):
            at, extra = cols[k]
            fill_tiles(
                table_ref, masks_ref, block_rows, ids_ref[at] + extra, rows // 128,
                lambda r: first_row + r, tblk // 128, tiles.at[pl.ds(k * rows, rows)],
            )
        total = jnp.dot(turned[...], tiles[...], preferred_element_type=F32)
        if has_acc:
            total = total + acc_ref[:, pl.ds(pl.multiple_of(begin, tblk), tblk)]
        out_ref[:, pl.ds(start, tblk)] = total.astype(out_ref.dtype)
        return carry

    lax.fori_loop(0, out_ref.shape[1] // tblk, block, 0)


def forward_mm(pieces, cols, side_at, ids, table, masks, acc, out_rows, tblk, block_rows, out_dtype, name):
    rows, width = pieces[0].shape
    count = len(pieces)
    args = [ids, table, masks] + list(pieces) + ([] if acc is None else [acc])
    turned = (width, count * rows)
    out_shape = [jax.ShapeDtypeStruct((width, out_rows), out_dtype)]
    scratch = [pltpu.VMEM((count * rows, tblk), BF16)]
    if acc is None:
        out_shape.append(jax.ShapeDtypeStruct(turned, BF16))
    else:
        scratch.insert(0, pltpu.VMEM(turned, BF16))
    return pl.pallas_call(
        partial(forward_kernel, tuple(cols), side_at, block_rows, tblk, acc is not None),
        in_specs=[smem_spec(), smem_spec()] + [vmem_spec()] * (len(args) - 2),
        out_specs=[vmem_spec()] * len(out_shape),
        scratch_shapes=scratch,
        out_shape=out_shape,
        compiler_params=pltpu.CompilerParams(vmem_limit_bytes=VMEM_LIMIT),
        cost_estimate=BRIEF,
        name=name,
    )(*args)


def shard_kernel(at, block_rows, ids_ref, table_ref, masks_ref, out_ref):
    fill_tiles(
        table_ref, masks_ref, block_rows, ids_ref[at], out_ref.shape[0] // 128,
        lambda r: r, block_rows, out_ref,
    )


def shard_tiles(at, node_rows, ids, table, masks, block_rows):
    return pl.pallas_call(
        partial(shard_kernel, at, block_rows),
        in_specs=[smem_spec(), smem_spec(), vmem_spec()],
        out_specs=vmem_spec(),
        out_shape=jax.ShapeDtypeStruct((node_rows, block_rows * 128), BF16),
        compiler_params=pltpu.CompilerParams(vmem_limit_bytes=VMEM_LIMIT),
        cost_estimate=BRIEF,
        name="far_tiles",
    )(ids, table, masks)


def last_kernel(at, ids_ref, tiles_ref, low_ref, high_ref, acc_ref, out_ref, turned):
    half = low_ref.shape[0]
    turned[:, :half] = low_ref[...].T
    turned[:, half:] = high_ref[...].T
    rows = out_ref.shape[1]
    columns = pl.ds(pl.multiple_of(ids_ref[at] * rows, rows), rows)
    total = jnp.dot(turned[...], tiles_ref[:, columns], preferred_element_type=F32)
    out_ref[...] = (total + acc_ref[:, columns]).astype(out_ref.dtype)


def last_forward(pieces, at, ids, tiles, acc, out_dtype, name):
    half, width = pieces[0].shape
    rows = acc.shape[1] // 2
    return pl.pallas_call(
        partial(last_kernel, at),
        in_specs=[smem_spec()] + [vmem_spec()] * 4,
        out_specs=vmem_spec(),
        out_shape=jax.ShapeDtypeStruct((width, rows), out_dtype),
        scratch_shapes=[pltpu.VMEM((width, 2 * half), BF16)],
        compiler_params=pltpu.CompilerParams(vmem_limit_bytes=VMEM_LIMIT),
        cost_estimate=BRIEF,
        name=name,
    )(ids, tiles, *pieces, acc)


def first_kernel(at, has_acc, ids_ref, tiles_ref, grad_ref, *refs):
    out_ref = refs[-1]
    rows = grad_ref.shape[0]
    columns = pl.ds(pl.multiple_of(ids_ref[at] * rows, rows), rows)
    total = jnp.dot(tiles_ref[:, columns], grad_ref[...], preferred_element_type=F32)
    if has_acc:
        total = total + refs[0][...]
    out_ref[...] = total.astype(out_ref.dtype)


def first_backward(grad, at, ids, tiles, acc, out_dtype, name):
    rows, width = grad.shape
    args = [ids, tiles, grad] + ([] if acc is None else [acc])
    return pl.pallas_call(
        partial(first_kernel, at, acc is not None),
        in_specs=[smem_spec()] + [vmem_spec()] * (len(args) - 1),
        out_specs=vmem_spec(),
        out_shape=jax.ShapeDtypeStruct((tiles.shape[0], width), out_dtype),
        compiler_params=pltpu.CompilerParams(vmem_limit_bytes=VMEM_LIMIT),
        cost_estimate=BRIEF,
        name=name,
    )(*args)


def middle_kernel(
    at, ids_ref, agg_ref, other_ref, div_ref, own_ref, og_ref, wn_ref, xt_ref,
    out_ref, gb_ref, mg_ref, keep_ref, send_ref,
):
    rows, width = own_ref.shape
    div = div_ref[...]
    mean_turned = (agg_ref[...] + other_ref[...].astype(F32)) / div
    mean = mean_turned.T.astype(BF16)
    pre = own_ref[...] + jnp.dot(mean, wn_ref[...], preferred_element_type=F32)
    square = pre * pre
    bent = jnp.tanh(GELU_C * (pre + 0.044715 * (square * pre)))
    half = 0.5 * (1.0 + bent)
    out_ref[...] = (pre * half).astype(BF16)
    slope = half + 0.5 * pre * (1.0 - bent * bent) * (GELU_C * (1.0 + 3.0 * 0.044715 * square))
    pre_grad = og_ref[...] * slope
    grad_b = pre_grad.astype(BF16)
    gb_ref[...] = grad_b
    div_column = jnp.broadcast_to(div, (128, rows)).T
    div_full = jnp.concatenate([div_column] * (width // 128), axis=1)
    mean_grad = lax.dot_general(
        grad_b, wn_ref[...], (((1,), (1,)), ((), ())), preferred_element_type=F32
    )
    mg_ref[...] = (mean_grad / div_full).astype(BF16)
    own = jnp.dot(xt_ref[...], grad_b, preferred_element_type=F32)
    neigh = jnp.dot(mean_turned.astype(BF16), grad_b, preferred_element_type=F32)
    first = ids_ref[at] == 0
    keep_ref[:width] = jnp.where(first, own, neigh)
    send_ref[:width] = jnp.where(first, neigh, own)
    bias = jnp.sum(pre_grad.reshape(rows // 64, 64, width), axis=0)
    keep_ref[width:] = bias
    send_ref[width:] = bias


def middle(at, ids, agg, other, divisor, own, og, wn, x_turned):
    rows, width = own.shape
    act = jax.ShapeDtypeStruct((rows, width), BF16)
    return pl.pallas_call(
        partial(middle_kernel, at),
        in_specs=[smem_spec()] + [vmem_spec()] * 7,
        out_specs=[vmem_spec()] * 5,
        out_shape=[act] * 3 + [jax.ShapeDtypeStruct((width + 64, width), F32)] * 2,
        compiler_params=pltpu.CompilerParams(vmem_limit_bytes=VMEM_LIMIT),
        cost_estimate=BRIEF,
        name="layer",
    )(ids, agg, other, divisor, own, og, wn, x_turned)


def cut_quarters(at, ids_ref, keep_ref, got_ref, outs):
    width = keep_ref.shape[1]
    rows, extra = width // 4, (keep_ref.shape[0] - width) // 4
    for x, out in enumerate(outs):
        quarter = ids_ref[at + x]
        for base, count, to in ((0, rows, 0), (width, extra, rows)):
            here = pl.ds(pl.multiple_of(base + quarter * count, 16), count)
            out[to : to + count] = (keep_ref[here] + got_ref[here]).astype(out.dtype)


def backward_kernel(cols, sides, block_rows, has_acc, cut_at, ids_ref, table_ref, masks_ref, after_ref, *refs):
    del after_ref
    grads = refs[: len(sides)]
    acc_ref = refs[len(sides)] if has_acc else None
    if cut_at is None:
        out_ref, tiles = refs[len(sides) + int(has_acc) :]
    else:
        keep_ref, got_ref, out_ref, *quarters, tiles = refs[len(sides) + int(has_acc) :]

        @pl.when(pl.program_id(0) == 0)
        def _():
            cut_quarters(cut_at, ids_ref, keep_ref, got_ref, quarters)

    piece_rows = out_ref.shape[0]
    rows = grads[0].shape[0]
    per_side = rows // 128
    first_col = ids_ref[cols[0]]
    for p in range(1, len(cols)):
        first_col = jnp.where(pl.program_id(0) == p, ids_ref[cols[p]], first_col)
    for k, side_at in enumerate(sides):
        base = ids_ref[side_at] * per_side
        fill_tiles(
            table_ref, masks_ref, block_rows, first_col, piece_rows // 128,
            lambda r: base + r, per_side, tiles.at[:, pl.ds(k * rows, rows)],
        )
    total = None
    for k in range(len(sides)):
        term = jnp.dot(
            tiles[:, k * rows : (k + 1) * rows], grads[k][...], preferred_element_type=F32
        )
        total = term if total is None else total + term
    if has_acc:
        total = total + acc_ref[...].astype(F32)
    out_ref[...] = total.astype(out_ref.dtype)


def backward_mm(cols, grads, sides, after, ids, table, masks, acc, piece_rows, block_rows, out_dtype, name,
    cut_at=None, weights=()):
    rows, width = grads[0].shape
    args = [ids, table, masks, after] + list(grads) + ([] if acc is None else [acc]) + list(weights)
    piece = pl.BlockSpec((piece_rows, width), lambda p: (p, 0))
    out_specs, out_shape = [piece], [jax.ShapeDtypeStruct((len(cols) * piece_rows, width), out_dtype)]
    if weights:
        quarter = (weights[0].shape[0] // 4, width)
        out_specs += [vmem_spec()] * 4
        out_shape += [jax.ShapeDtypeStruct(quarter, F32)] + [jax.ShapeDtypeStruct(quarter, BF16)] * 3
    outs = pl.pallas_call(
        partial(backward_kernel, tuple(cols), tuple(sides), block_rows, acc is not None, cut_at),
        grid=(len(cols),),
        in_specs=[smem_spec(), smem_spec(), vmem_spec(), pl.BlockSpec(memory_space=pl.ANY)]
        + [vmem_spec()] * len(grads)
        + ([] if acc is None else [piece])
        + [vmem_spec()] * len(weights),
        out_specs=out_specs,
        scratch_shapes=[pltpu.VMEM((piece_rows, len(grads) * rows), BF16)],
        out_shape=out_shape,
        compiler_params=pltpu.CompilerParams(vmem_limit_bytes=VMEM_LIMIT),
        cost_estimate=pl.CostEstimate(
            flops=8 * len(cols) * piece_rows * rows * len(grads) * width,
            bytes_accessed=masks.size * 4 + 4 * len(cols) * piece_rows * width,
            transcendentals=0,
        ),
        name=name,
    )(*args)
    return outs if weights else outs[0]


def small_call(kernel, name, out_shape, args, scratch=()):
    return pl.pallas_call(
        kernel,
        in_specs=[smem_spec()] + [vmem_spec()] * (len(args) - 1),
        out_specs=[vmem_spec()] * len(out_shape),
        out_shape=out_shape,
        scratch_shapes=list(scratch),
        compiler_params=pltpu.CompilerParams(vmem_limit_bytes=VMEM_LIMIT),
        cost_estimate=BRIEF,
        name=name,
    )(*args)


def join_kernel(at, ids_ref, *refs):
    parts, (matrix_ref, bias_ref) = refs[:-2], refs[-2:]
    rows, extra = matrix_ref.shape[0] // 4, bias_ref.shape[0] // 4
    for x, part in enumerate(parts):
        quarter = ids_ref[at + x]
        matrix_ref[pl.ds(pl.multiple_of(quarter * rows, 16), rows)] = part[:rows]
        bias_ref[pl.ds(pl.multiple_of(quarter * extra, 16), extra)] = part[rows:]


def scale_kernel(at, scale, ids_ref, own_ref, got_ref, bias_ref, self_ref, neigh_ref, sum_ref):
    first = ids_ref[at] == 0
    own, got = own_ref[...].astype(F32) * scale, got_ref[...].astype(F32) * scale
    self_ref[...] = jnp.where(first, own, got)
    neigh_ref[...] = jnp.where(first, got, own)
    sum_ref[...] = jnp.sum(bias_ref[...].astype(F32), axis=0, keepdims=True) * scale


def local(
    node_features, tile_rows, tile_cols, tile_masks, tile_count,
    weight_self, weight_neigh, bias_term, out_grad,
):
    node_rows, width = node_features.shape
    n = lax.axis_size("row")
    grid_cols = lax.axis_size("col")
    slots = tile_masks.shape[2]
    block_rows = grid_cols * node_rows // 128
    block_cols = n * node_rows // 128
    half = node_rows // 2
    far = n // 2

    order = ring_order(n)
    clockwise = [(order[k], order[(k + 1) % n]) for k in range(n)]
    counter = [(b, a) for a, b in clockwise]
    swap = [(0, 1), (1, 0)]
    row_id = lax.axis_index("row")
    side = lax.axis_index("col").astype(jnp.int32)
    shard_cols = node_rows // 128
    at_side, at_other, at_quad = n, n + 1, n + 2
    known = [
        [order[(order.index(r) + k) % n] * shard_cols for k in range(n)]
        + [c, 1 - c]
        + [(r & 3) ^ x for x in range(4)]
        for r in range(n)
        for c in range(grid_cols)
    ]
    ids = lax.dynamic_index_in_dim(
        jnp.array(known, jnp.int32), row_id * grid_cols + side, 0, keepdims=False
    )

    row_index = tile_rows.reshape(slots)
    col_index = tile_cols.reshape(slots)
    masks = jnp.transpose(tile_masks.reshape(slots, 128, 8), (0, 2, 1))
    slot_ids = jnp.arange(slots, dtype=jnp.int32)
    live = slot_ids < tile_count.reshape(())
    keys = jnp.where(live, col_index * block_rows + row_index, -1)
    spots = jnp.arange(block_rows * block_cols, dtype=jnp.int32)
    table = jnp.max(jnp.where(keys[None, :] == spots[:, None], slot_ids[None, :], -1), axis=1)
    counts = jnp.sum(lax.population_count(masks), axis=1).astype(BF16)
    pick = ((jnp.arange(block_rows, dtype=jnp.int32)[:, None] == row_index[None, :]) & live[None, :])
    degree = jnp.dot(pick.astype(BF16), counts, preferred_element_type=F32).reshape(2, 1, node_rows)
    sent_degree = lax.ppermute(lax.dynamic_index_in_dim(degree, 1 - side, 0, False), "col", swap)
    degree = lax.dynamic_index_in_dim(degree, side, 0, False) + sent_degree
    divisor = jnp.maximum(degree, 1.0)

    row_total = block_rows * 128
    forward = partial(forward_mm, ids=ids, table=table, masks=masks, block_rows=block_rows, tblk=1024)
    from_left = from_right = node_features
    pieces, cols, acc = [node_features], [(0, 0)], None
    early = (node_features, weight_self, bias_term, out_grad, ids, divisor)
    for s in range(1, far + 1):
        if s < far:
            next_left = lax.ppermute(from_left, "row", clockwise)
            next_right = lax.ppermute(from_right, "row", counter)
            next_cols = [(n - s, 0), (s, 0)]
        else:
            next_left = lax.ppermute(from_left[:half], "row", clockwise)
            next_right = lax.ppermute(from_right[half:], "row", counter)
        acc, *rest = forward(
            pieces, cols, None, acc=acc, out_rows=row_total, out_dtype=F32, name="forward_step"
        )
        x_turned = rest[0] if rest else x_turned
        if s == 2:
            x_now, ws_now, b_now, og_now, ids_now, div_now = early
            own_part = jnp.dot(x_now, ws_now, preferred_element_type=F32) + b_now
            far_tiles = shard_tiles(far, node_rows, ids_now, table, masks, block_rows)
            early = (own_part, og_now.astype(F32), far_tiles, div_now)
        acc, from_left, early = lax.optimization_barrier((acc, next_left, early))
        acc, from_right = lax.optimization_barrier((acc, next_right))
        pieces, cols = [from_left, from_right], next_cols
    own_part, wide_out_grad, far_tiles, divisor = early
    for_other = last_forward(pieces, at_other, ids, far_tiles, acc, BF16, "forward_send")
    received = lax.ppermute(for_other, "col", swap)
    mine = last_forward(pieces, at_side, ids, far_tiles, acc, F32, "forward_keep")
    mine, received = lax.optimization_barrier((mine, received))

    node_out, grad_b, mean_grad, keep, sent = middle(
        at_side, ids, mine, received, divisor, own_part, wide_out_grad, weight_neigh, x_turned
    )
    other_grad = lax.ppermute(mean_grad, "col", swap)

    backward = partial(
        backward_mm, ids=ids, table=table, masks=masks, piece_rows=node_rows, block_rows=block_rows
    )
    far_terms = first_backward(mean_grad, at_side, ids, far_tiles, None, F32, "backward_far_own")
    far_terms = first_backward(other_grad, at_other, ids, far_tiles, far_terms, BF16, "backward_far")
    both_grads, both_sides = [mean_grad, other_grad], [at_side, at_other]

    grad_scale = (node_rows * n * grid_cols) ** (-0.5)
    bits = int(math.log2(n))

    def array(rows, dtype):
        return jax.ShapeDtypeStruct((rows, width), dtype)

    def to_quad(parts, axis="row"):
        return [lax.ppermute(part, axis, [(r, r ^ x) for r in range(n)]) for x, part in parts]

    def start_quad(parts):
        return [parts[0]] + to_quad(list(enumerate(parts[1:], 1)))

    def rounded_sum(parts):
        total = parts[0].astype(F32)
        for part in parts[1:]:
            total = total + part.astype(F32)
        return total.astype(BF16)

    def add_all(b, parts):
        quarter = rounded_sum(parts)
        return [quarter, lax.ppermute(quarter, "row", [(r, r ^ (1 << b)) for r in range(n)])]

    def from_quad(parts):
        quarter = rounded_sum(parts)
        return [quarter] + to_quad([(x, quarter) for x in (1, 2, 3)])

    spread = [[] for _ in range(far)]
    spread[0].append(start_quad)
    for b in range(2, bits):
        spread[b - 1].append(partial(add_all, b))
    spread[bits - 1].append(from_quad)

    weights = (keep, lax.ppermute(sent, "col", swap))
    right, left = far_terms[:half], far_terms[half:]
    for s in range(far - 1, -1, -1):
        mean_grad, other_grad = both_grads
        right, mean_grad = lax.optimization_barrier((right, mean_grad))
        left, other_grad = lax.optimization_barrier((left, other_grad))
        grads = [mean_grad, other_grad]
        right = lax.ppermute(right, "row", clockwise)
        left = lax.ppermute(left, "row", counter)
        if s > 0:
            first = s == far - 1
            terms = backward(
                [s, n - s], grads, both_sides, grads[0], acc=None, out_dtype=BF16, name="backward_step",
                cut_at=at_quad if first else None, weights=weights if first else (),
            )
            if first:
                terms, *weights = terms
        else:
            terms = backward(
                [0], grads, both_sides, grads[0], acc=None, out_dtype=F32, name="backward_own"
            )
            self_term = lax.dot_general(
                grad_b, weight_self, (((1,), (1,)), ((), ())), preferred_element_type=F32
            )
            terms = terms + self_term
        terms, weights = lax.optimization_barrier((terms, weights))
        for one in spread[far - 1 - s]:
            weights = one(weights)
        terms, both_grads = lax.optimization_barrier((terms, grads))
        if s > 0:
            if s == far - 1:
                gap = jnp.zeros((half, width), BF16)
                right = jnp.concatenate([right, gap], axis=0)
                left = jnp.concatenate([gap, left], axis=0)
            right = (terms[:node_rows].astype(F32) + right.astype(F32)).astype(BF16)
            left = (terms[node_rows:].astype(F32) + left.astype(F32)).astype(BF16)
        else:
            feature_grad = (terms + right.astype(F32) + left.astype(F32)).astype(BF16)

    matrix, bias_sums = small_call(
        partial(join_kernel, at_quad), "join_grads", [array(width, BF16), array(64, BF16)],
        (ids,) + tuple(weights),
    )
    got = lax.ppermute(matrix, "col", swap)
    grad_self, grad_neigh, grad_bias = small_call(
        partial(scale_kernel, at_side, grad_scale), "scale_grads",
        [array(width, F32)] * 2 + [array(1, F32)], (ids, matrix, got, bias_sums),
    )
    grad_bias = grad_bias.reshape(width)
    return node_out, feature_grad, grad_self, grad_neigh, grad_bias


def solution(mesh):
    in_specs = (
        P(("groups", "row", "col"), None),
        P(("groups", "row"), "col", None),
        P(("groups", "row"), "col", None),
        P(("groups", "row"), "col", None, None, None),
        P(("groups", "row"), "col"),
        P(),
        P(),
        P(),
        P(("groups", "row", "col"), None),
    )
    out_specs = (
        P(("groups", "row", "col"), None),
        P(("groups", "row", "col"), None),
        P("groups", None),
        P("groups", None),
        P("groups"),
    )
    return jax.shard_map(local, mesh=mesh, in_specs=in_specs, out_specs=out_specs, check_vma=False)
```

```python
from functools import partial
import math

import jax
import jax.numpy as jnp
from jax import lax
from jax.experimental import pallas as pl
from jax.experimental.pallas import tpu as pltpu
from jax.sharding import PartitionSpec as P

VMEM_LIMIT = 14 * 1024 * 1024
BRIEF = pl.CostEstimate(flops=1024, bytes_accessed=1024, transcendentals=0)
GELU_C = math.sqrt(2.0 / math.pi)
F32 = jnp.float32
BF16 = jnp.bfloat16


def ring_order(n):
    return list(range(0, n, 2)) + list(range(n - 1, 0, -2))


def unpack_tile(masks_ref, slot, test):
    words = masks_ref[jnp.maximum(slot, 0)]
    words = jnp.where(slot >= 0, words, 0)
    one, zero = jnp.ones((), BF16), jnp.zeros((), BF16)
    parts = []
    for k in range(8):
        row = jnp.broadcast_to(words[k : k + 1, :], (16, 128)).astype(jnp.int16)
        parts.append(jnp.where(jnp.bitwise_and(row, test) != 0, one, zero))
    return jnp.concatenate(parts, axis=0)


def bit_tests():
    return jnp.left_shift(jnp.ones((), jnp.int16), lax.broadcasted_iota(jnp.int16, (16, 128), 0))


def fill_tiles(table_ref, masks_ref, block_rows, first_col, cols, row_of, tiles, dst):
    test = bit_tests()

    for c in range(cols):
        base = (first_col + c) * block_rows
        for r in range(tiles):
            tile = unpack_tile(masks_ref, table_ref[base + row_of(r)], test)
            dst[128 * c : 128 * c + 128, 128 * r : 128 * r + 128] = tile


def vmem_spec():
    return pl.BlockSpec(memory_space=pltpu.VMEM)


def smem_spec():
    return pl.BlockSpec(memory_space=pltpu.SMEM)


def forward_kernel(cols, side_at, block_rows, tblk, has_acc, ids_ref, table_ref, masks_ref, *refs):
    count = len(cols)
    xs = refs[:count]
    acc_ref = refs[count] if has_acc else None
    out_ref, turned, tiles = refs[count + int(has_acc) :]
    rows = xs[0].shape[0]
    for k in range(count):
        turned[:, k * rows : (k + 1) * rows] = xs[k][...].T
    first = ids_ref[side_at] * out_ref.shape[1] if side_at is not None else 0

    def block(q, carry):
        start = pl.multiple_of(q * tblk, tblk)
        begin = first + start
        first_row = begin // 128
        for k in range(count):
            at, extra = cols[k]
            fill_tiles(
                table_ref, masks_ref, block_rows, ids_ref[at] + extra, rows // 128,
                lambda r: first_row + r, tblk // 128, tiles.at[pl.ds(k * rows, rows)],
            )
        total = jnp.dot(turned[...], tiles[...], preferred_element_type=F32)
        if has_acc:
            total = total + acc_ref[:, pl.ds(pl.multiple_of(begin, tblk), tblk)]
        out_ref[:, pl.ds(start, tblk)] = total.astype(out_ref.dtype)
        return carry

    lax.fori_loop(0, out_ref.shape[1] // tblk, block, 0)


def forward_mm(pieces, cols, side_at, ids, table, masks, acc, out_rows, tblk, block_rows, out_dtype, name):
    rows, width = pieces[0].shape
    count = len(pieces)
    args = [ids, table, masks] + list(pieces) + ([] if acc is None else [acc])
    turned = (width, count * rows)
    out_shape = [jax.ShapeDtypeStruct((width, out_rows), out_dtype)]
    scratch = [pltpu.VMEM((count * rows, tblk), BF16)]
    if acc is None:
        out_shape.append(jax.ShapeDtypeStruct(turned, BF16))
    else:
        scratch.insert(0, pltpu.VMEM(turned, BF16))
    return pl.pallas_call(
        partial(forward_kernel, tuple(cols), side_at, block_rows, tblk, acc is not None),
        in_specs=[smem_spec(), smem_spec()] + [vmem_spec()] * (len(args) - 2),
        out_specs=[vmem_spec()] * len(out_shape),
        scratch_shapes=scratch,
        out_shape=out_shape,
        compiler_params=pltpu.CompilerParams(vmem_limit_bytes=VMEM_LIMIT),
        cost_estimate=BRIEF,
        name=name,
    )(*args)


def shard_kernel(at, block_rows, ids_ref, table_ref, masks_ref, out_ref):
    fill_tiles(
        table_ref, masks_ref, block_rows, ids_ref[at], out_ref.shape[0] // 128,
        lambda r: r, block_rows, out_ref,
    )


def shard_tiles(at, node_rows, ids, table, masks, block_rows):
    return pl.pallas_call(
        partial(shard_kernel, at, block_rows),
        in_specs=[smem_spec(), smem_spec(), vmem_spec()],
        out_specs=vmem_spec(),
        out_shape=jax.ShapeDtypeStruct((node_rows, block_rows * 128), BF16),
        compiler_params=pltpu.CompilerParams(vmem_limit_bytes=VMEM_LIMIT),
        cost_estimate=BRIEF,
        name="far_tiles",
    )(ids, table, masks)


def last_kernel(at, ids_ref, tiles_ref, low_ref, high_ref, acc_ref, out_ref, turned):
    half = low_ref.shape[0]
    turned[:, :half] = low_ref[...].T
    turned[:, half:] = high_ref[...].T
    rows = out_ref.shape[1]
    columns = pl.ds(pl.multiple_of(ids_ref[at] * rows, rows), rows)
    total = jnp.dot(turned[...], tiles_ref[:, columns], preferred_element_type=F32)
    out_ref[...] = (total + acc_ref[:, columns]).astype(out_ref.dtype)


def last_forward(pieces, at, ids, tiles, acc, out_dtype, name):
    half, width = pieces[0].shape
    rows = acc.shape[1] // 2
    return pl.pallas_call(
        partial(last_kernel, at),
        in_specs=[smem_spec()] + [vmem_spec()] * 4,
        out_specs=vmem_spec(),
        out_shape=jax.ShapeDtypeStruct((width, rows), out_dtype),
        scratch_shapes=[pltpu.VMEM((width, 2 * half), BF16)],
        compiler_params=pltpu.CompilerParams(vmem_limit_bytes=VMEM_LIMIT),
        cost_estimate=BRIEF,
        name=name,
    )(ids, tiles, *pieces, acc)


def first_kernel(at, has_acc, ids_ref, tiles_ref, grad_ref, *refs):
    out_ref = refs[-1]
    rows = grad_ref.shape[0]
    columns = pl.ds(pl.multiple_of(ids_ref[at] * rows, rows), rows)
    total = jnp.dot(tiles_ref[:, columns], grad_ref[...], preferred_element_type=F32)
    if has_acc:
        total = total + refs[0][...]
    out_ref[...] = total.astype(out_ref.dtype)


def first_backward(grad, at, ids, tiles, acc, out_dtype, name):
    rows, width = grad.shape
    args = [ids, tiles, grad] + ([] if acc is None else [acc])
    return pl.pallas_call(
        partial(first_kernel, at, acc is not None),
        in_specs=[smem_spec()] + [vmem_spec()] * (len(args) - 1),
        out_specs=vmem_spec(),
        out_shape=jax.ShapeDtypeStruct((tiles.shape[0], width), out_dtype),
        compiler_params=pltpu.CompilerParams(vmem_limit_bytes=VMEM_LIMIT),
        cost_estimate=BRIEF,
        name=name,
    )(*args)


def middle_kernel(
    at, ids_ref, agg_ref, other_ref, div_ref, own_ref, og_ref, wn_ref, xt_ref,
    out_ref, gb_ref, mg_ref, keep_ref, send_ref,
):
    rows, width = own_ref.shape
    div = div_ref[...]
    mean_turned = (agg_ref[...] + other_ref[...].astype(F32)) / div
    mean = mean_turned.T.astype(BF16)
    pre = own_ref[...] + jnp.dot(mean, wn_ref[...], preferred_element_type=F32)
    square = pre * pre
    bent = jnp.tanh(GELU_C * (pre + 0.044715 * (square * pre)))
    half = 0.5 * (1.0 + bent)
    out_ref[...] = (pre * half).astype(BF16)
    slope = half + 0.5 * pre * (1.0 - bent * bent) * (GELU_C * (1.0 + 3.0 * 0.044715 * square))
    pre_grad = og_ref[...] * slope
    grad_b = pre_grad.astype(BF16)
    gb_ref[...] = grad_b
    div_column = jnp.broadcast_to(div, (128, rows)).T
    div_full = jnp.concatenate([div_column] * (width // 128), axis=1)
    mean_grad = lax.dot_general(
        grad_b, wn_ref[...], (((1,), (1,)), ((), ())), preferred_element_type=F32
    )
    mg_ref[...] = (mean_grad / div_full).astype(BF16)
    own = jnp.dot(xt_ref[...], grad_b, preferred_element_type=F32)
    neigh = jnp.dot(mean_turned.astype(BF16), grad_b, preferred_element_type=F32)
    first = ids_ref[at] == 0
    keep_ref[:width] = jnp.where(first, own, neigh)
    send_ref[:width] = jnp.where(first, neigh, own)
    bias = jnp.sum(pre_grad.reshape(rows // 64, 64, width), axis=0)
    keep_ref[width:] = bias
    send_ref[width:] = bias


def middle(at, ids, agg, other, divisor, own, og, wn, x_turned):
    rows, width = own.shape
    act = jax.ShapeDtypeStruct((rows, width), BF16)
    return pl.pallas_call(
        partial(middle_kernel, at),
        in_specs=[smem_spec()] + [vmem_spec()] * 7,
        out_specs=[vmem_spec()] * 5,
        out_shape=[act] * 3 + [jax.ShapeDtypeStruct((width + 64, width), F32)] * 2,
        compiler_params=pltpu.CompilerParams(vmem_limit_bytes=VMEM_LIMIT),
        cost_estimate=BRIEF,
        name="layer",
    )(ids, agg, other, divisor, own, og, wn, x_turned)


def backward_kernel(cols, sides, block_rows, has_acc, ids_ref, table_ref, masks_ref, after_ref, *refs):
    del after_ref
    grads = refs[: len(sides)]
    acc_ref = refs[len(sides)] if has_acc else None
    out_ref, tiles = refs[len(sides) + int(has_acc) :]
    piece_rows = out_ref.shape[0]
    rows = grads[0].shape[0]
    per_side = rows // 128
    first_col = ids_ref[cols[0]]
    for p in range(1, len(cols)):
        first_col = jnp.where(pl.program_id(0) == p, ids_ref[cols[p]], first_col)
    for k, side_at in enumerate(sides):
        base = ids_ref[side_at] * per_side
        fill_tiles(
            table_ref, masks_ref, block_rows, first_col, piece_rows // 128,
            lambda r: base + r, per_side, tiles.at[:, pl.ds(k * rows, rows)],
        )
    total = None
    for k in range(len(sides)):
        term = jnp.dot(
            tiles[:, k * rows : (k + 1) * rows], grads[k][...], preferred_element_type=F32
        )
        total = term if total is None else total + term
    if has_acc:
        total = total + acc_ref[...].astype(F32)
    out_ref[...] = total.astype(out_ref.dtype)


def backward_mm(cols, grads, sides, after, ids, table, masks, acc, piece_rows, block_rows, out_dtype, name):
    rows, width = grads[0].shape
    args = [ids, table, masks, after] + list(grads) + ([] if acc is None else [acc])
    piece = pl.BlockSpec((piece_rows, width), lambda p: (p, 0))
    return pl.pallas_call(
        partial(backward_kernel, tuple(cols), tuple(sides), block_rows, acc is not None),
        grid=(len(cols),),
        in_specs=[smem_spec(), smem_spec(), vmem_spec(), pl.BlockSpec(memory_space=pl.ANY)]
        + [vmem_spec()] * len(grads)
        + ([] if acc is None else [piece]),
        out_specs=piece,
        scratch_shapes=[pltpu.VMEM((piece_rows, len(grads) * rows), BF16)],
        out_shape=jax.ShapeDtypeStruct((len(cols) * piece_rows, width), out_dtype),
        compiler_params=pltpu.CompilerParams(vmem_limit_bytes=VMEM_LIMIT),
        cost_estimate=pl.CostEstimate(
            flops=8 * len(cols) * piece_rows * rows * len(grads) * width,
            bytes_accessed=masks.size * 4 + 4 * len(cols) * piece_rows * width,
            transcendentals=0,
        ),
        name=name,
    )(*args)


def small_call(kernel, name, out_shape, args, scratch=()):
    return pl.pallas_call(
        kernel,
        in_specs=[smem_spec()] + [vmem_spec()] * (len(args) - 1),
        out_specs=[vmem_spec()] * len(out_shape),
        out_shape=out_shape,
        scratch_shapes=list(scratch),
        compiler_params=pltpu.CompilerParams(vmem_limit_bytes=VMEM_LIMIT),
        cost_estimate=BRIEF,
        name=name,
    )(*args)


def quarter_kernel(at, ids_ref, keep_ref, got_ref, own_ref, *sends):
    extra = keep_ref.shape[0] - 256 * (keep_ref.shape[0] // 256)
    rows, extra = (keep_ref.shape[0] - extra) // 4, extra // 4
    for x, out in enumerate((own_ref,) + sends):
        quarter = ids_ref[at + x]
        for base, count, to in ((0, rows, 0), (4 * rows, extra, rows)):
            here = pl.ds(pl.multiple_of(base + quarter * count, 16), count)
            out[to : to + count] = (keep_ref[here] + got_ref[here]).astype(out.dtype)


def join_kernel(at, ids_ref, *refs):
    parts, (matrix_ref, bias_ref) = refs[:-2], refs[-2:]
    rows, extra = matrix_ref.shape[0] // 4, bias_ref.shape[0] // 4
    for x, part in enumerate(parts):
        quarter = ids_ref[at + x]
        matrix_ref[pl.ds(pl.multiple_of(quarter * rows, 16), rows)] = part[:rows]
        bias_ref[pl.ds(pl.multiple_of(quarter * extra, 16), extra)] = part[rows:]


def scale_kernel(at, scale, ids_ref, own_ref, got_ref, bias_ref, self_ref, neigh_ref, sum_ref):
    first = ids_ref[at] == 0
    own, got = own_ref[...].astype(F32) * scale, got_ref[...].astype(F32) * scale
    self_ref[...] = jnp.where(first, own, got)
    neigh_ref[...] = jnp.where(first, got, own)
    sum_ref[...] = jnp.sum(bias_ref[...].astype(F32), axis=0, keepdims=True) * scale


def local(
    node_features, tile_rows, tile_cols, tile_masks, tile_count,
    weight_self, weight_neigh, bias_term, out_grad,
):
    node_rows, width = node_features.shape
    n = lax.axis_size("row")
    grid_cols = lax.axis_size("col")
    slots = tile_masks.shape[2]
    block_rows = grid_cols * node_rows // 128
    block_cols = n * node_rows // 128
    half = node_rows // 2
    far = n // 2

    order = ring_order(n)
    clockwise = [(order[k], order[(k + 1) % n]) for k in range(n)]
    counter = [(b, a) for a, b in clockwise]
    swap = [(0, 1), (1, 0)]
    row_id = lax.axis_index("row")
    side = lax.axis_index("col").astype(jnp.int32)
    shard_cols = node_rows // 128
    at_side, at_other, at_quad = n, n + 1, n + 2
    known = [
        [order[(order.index(r) + k) % n] * shard_cols for k in range(n)]
        + [c, 1 - c]
        + [(r & 3) ^ x for x in range(4)]
        for r in range(n)
        for c in range(grid_cols)
    ]
    ids = lax.dynamic_index_in_dim(
        jnp.array(known, jnp.int32), row_id * grid_cols + side, 0, keepdims=False
    )

    row_index = tile_rows.reshape(slots)
    col_index = tile_cols.reshape(slots)
    masks = jnp.transpose(tile_masks.reshape(slots, 128, 8), (0, 2, 1))
    slot_ids = jnp.arange(slots, dtype=jnp.int32)
    live = slot_ids < tile_count.reshape(())
    keys = jnp.where(live, col_index * block_rows + row_index, -1)
    spots = jnp.arange(block_rows * block_cols, dtype=jnp.int32)
    table = jnp.max(jnp.where(keys[None, :] == spots[:, None], slot_ids[None, :], -1), axis=1)
    counts = jnp.sum(lax.population_count(masks), axis=1).astype(BF16)
    pick = ((jnp.arange(block_rows, dtype=jnp.int32)[:, None] == row_index[None, :]) & live[None, :])
    degree = jnp.dot(pick.astype(BF16), counts, preferred_element_type=F32).reshape(2, 1, node_rows)
    sent_degree = lax.ppermute(lax.dynamic_index_in_dim(degree, 1 - side, 0, False), "col", swap)
    degree = lax.dynamic_index_in_dim(degree, side, 0, False) + sent_degree
    divisor = jnp.maximum(degree, 1.0)

    row_total = block_rows * 128
    forward = partial(forward_mm, ids=ids, table=table, masks=masks, block_rows=block_rows, tblk=1024)
    from_left = from_right = node_features
    pieces, cols, acc = [node_features], [(0, 0)], None
    early = (node_features, weight_self, bias_term, out_grad, ids, divisor)
    for s in range(1, far + 1):
        if s < far:
            next_left = lax.ppermute(from_left, "row", clockwise)
            next_right = lax.ppermute(from_right, "row", counter)
            next_cols = [(n - s, 0), (s, 0)]
        else:
            next_left = lax.ppermute(from_left[:half], "row", clockwise)
            next_right = lax.ppermute(from_right[half:], "row", counter)
        acc, *rest = forward(
            pieces, cols, None, acc=acc, out_rows=row_total, out_dtype=F32, name="forward_step"
        )
        x_turned = rest[0] if rest else x_turned
        if s == 2:
            x_now, ws_now, b_now, og_now, ids_now, div_now = early
            own_part = jnp.dot(x_now, ws_now, preferred_element_type=F32) + b_now
            far_tiles = shard_tiles(far, node_rows, ids_now, table, masks, block_rows)
            early = (own_part, og_now.astype(F32), far_tiles, div_now)
        acc, from_left, early = lax.optimization_barrier((acc, next_left, early))
        acc, from_right = lax.optimization_barrier((acc, next_right))
        pieces, cols = [from_left, from_right], next_cols
    own_part, wide_out_grad, far_tiles, divisor = early
    for_other = last_forward(pieces, at_other, ids, far_tiles, acc, BF16, "forward_send")
    received = lax.ppermute(for_other, "col", swap)
    mine = last_forward(pieces, at_side, ids, far_tiles, acc, F32, "forward_keep")
    mine, received = lax.optimization_barrier((mine, received))

    node_out, grad_b, mean_grad, keep, sent = middle(
        at_side, ids, mine, received, divisor, own_part, wide_out_grad, weight_neigh, x_turned
    )
    other_grad = lax.ppermute(mean_grad, "col", swap)

    backward = partial(
        backward_mm, ids=ids, table=table, masks=masks, piece_rows=node_rows, block_rows=block_rows
    )
    far_terms = first_backward(mean_grad, at_side, ids, far_tiles, None, F32, "backward_far_own")
    far_terms = first_backward(other_grad, at_other, ids, far_tiles, far_terms, BF16, "backward_far")
    both_grads, both_sides = [mean_grad, other_grad], [at_side, at_other]

    grad_scale = (node_rows * n * grid_cols) ** (-0.5)
    bits = int(math.log2(n))

    def array(rows, dtype):
        return jax.ShapeDtypeStruct((rows, width), dtype)

    def to_quad(parts, axis="row"):
        sent = {
            x: lax.ppermute(part, axis, [(r, r ^ x) for r in range(n)]) for x, part in reversed(parts)
        }
        return [sent[x] for x, _ in parts]

    def start_quad(parts):
        own, *sends = small_call(
            partial(quarter_kernel, at_quad), "weight_quarters",
            [array(width // 4 + 16, F32)] + [array(width // 4 + 16, BF16)] * 3, (ids,) + parts,
        )
        return [own] + to_quad(list(enumerate(sends, 1)))

    def rounded_sum(parts):
        total = parts[0].astype(F32)
        for part in parts[1:]:
            total = total + part.astype(F32)
        return total.astype(BF16)

    def add_all(b, parts):
        quarter = rounded_sum(parts)
        return [quarter, lax.ppermute(quarter, "row", [(r, r ^ (1 << b)) for r in range(n)])]

    def from_quad(parts):
        quarter = rounded_sum(parts)
        return [quarter] + to_quad([(x, quarter) for x in (1, 2, 3)])

    spread = [[] for _ in range(far)]
    spread[0].append(start_quad)
    for b in range(2, bits):
        spread[b - 1].append(partial(add_all, b))
    spread[bits - 1].append(from_quad)

    weights = (keep, lax.ppermute(sent, "col", swap))
    right, left = far_terms[:half], far_terms[half:]
    for s in range(far - 1, -1, -1):
        mean_grad, other_grad = both_grads
        right, mean_grad = lax.optimization_barrier((right, mean_grad))
        left, other_grad = lax.optimization_barrier((left, other_grad))
        grads = [mean_grad, other_grad]
        right = lax.ppermute(right, "row", clockwise)
        left = lax.ppermute(left, "row", counter)
        if s > 0:
            terms = backward(
                [s, n - s], grads, both_sides, grads[0], acc=None, out_dtype=BF16, name="backward_step"
            )
        else:
            terms = backward(
                [0], grads, both_sides, grads[0], acc=None, out_dtype=F32, name="backward_own"
            )
            self_term = lax.dot_general(
                grad_b, weight_self, (((1,), (1,)), ((), ())), preferred_element_type=F32
            )
            terms = terms + self_term
        terms, weights = lax.optimization_barrier((terms, weights))
        for one in spread[far - 1 - s]:
            weights = one(weights)
        terms, both_grads = lax.optimization_barrier((terms, grads))
        if s > 0:
            if s == far - 1:
                gap = jnp.zeros((half, width), BF16)
                right = jnp.concatenate([right, gap], axis=0)
                left = jnp.concatenate([gap, left], axis=0)
            right = (terms[:node_rows].astype(F32) + right.astype(F32)).astype(BF16)
            left = (terms[node_rows:].astype(F32) + left.astype(F32)).astype(BF16)
        else:
            feature_grad = (terms + right.astype(F32) + left.astype(F32)).astype(BF16)

    matrix, bias_sums = small_call(
        partial(join_kernel, at_quad), "join_grads", [array(width, BF16), array(64, BF16)],
        (ids,) + tuple(weights),
    )
    got = lax.ppermute(matrix, "col", swap)
    grad_self, grad_neigh, grad_bias = small_call(
        partial(scale_kernel, at_side, grad_scale), "scale_grads",
        [array(width, F32)] * 2 + [array(1, F32)], (ids, matrix, got, bias_sums),
    )
    grad_bias = grad_bias.reshape(width)
    return node_out, feature_grad, grad_self, grad_neigh, grad_bias


def solution(mesh):
    in_specs = (
        P(("groups", "row", "col"), None),
        P(("groups", "row"), "col", None),
        P(("groups", "row"), "col", None),
        P(("groups", "row"), "col", None, None, None),
        P(("groups", "row"), "col"),
        P(),
        P(),
        P(),
        P(("groups", "row", "col"), None),
    )
    out_specs = (
        P(("groups", "row", "col"), None),
        P(("groups", "row", "col"), None),
        P("groups", None),
        P("groups", None),
        P("groups"),
    )
    return jax.shard_map(local, mesh=mesh, in_specs=in_specs, out_specs=out_specs, check_vma=False)
```
